32 devices in a mesh: ctx: 8 (over y, x, core), head: 4 (over z).
Axes of the slice: x: 2, y: 2, z: 4, core: 2. Of those that a mesh axis runs over, the one named last changes fastest.
Arguments:
- queries: bfloat16 [1024, 8192], P('ctx', 'head'), may hold values from -6 to 6
- keys_in: bfloat16 [1024, 1024], P('ctx', 'head'), may hold values from -6 to 6
- values_in: bfloat16 [1024, 1024], P('ctx', 'head'), may hold values from -6 to 6
- attn_cotan: bfloat16 [1024, 8192], P('ctx', 'head'), may hold values from -6 to 6
- doc_ids: int32 [1024], P('ctx'), may hold values from 0 to 5, never falling along the last dimension, each value on 1 to 512 neighbouring positions
- ssd_input: bfloat16 [1024, 16384], P('ctx', 'head'), may hold values from -0.29882812 to 0.29882812
- state_write: bfloat16 [1024, 256], P('ctx'), may hold values from -0.375 to 0.375
- state_read: bfloat16 [1024, 256], P('ctx'), may hold values from -6 to 6
- log_decay: float32 [1024, 256], P('ctx', 'head'), may hold values from -1.3 to 0
- ssd_cotan: bfloat16 [1024, 16384], P('ctx', 'head'), may hold values from -0.119628906 to 0.119628906
Outputs:
- attn_out: bfloat16 [1024, 8192], P('ctx', 'head')
- ssd_out: bfloat16 [1024, 16384], P('ctx', 'head')
- grad_q: bfloat16 [1024, 8192], P('ctx', 'head')
- grad_k: bfloat16 [1024, 1024], P('ctx', 'head')
- grad_v: bfloat16 [1024, 1024], P('ctx', 'head')
- grad_x: bfloat16 [1024, 16384], P('ctx', 'head')
- grad_b: bfloat16 [1024, 256], P(('ctx', 'head'))
- grad_c: bfloat16 [1024, 256], P(('ctx', 'head'))
The draws below stay inside these ranges and needn't reach their ends.
Inputs may be any that keep to these rules, and one draw needn't show every extreme that they name: doc_ids never fall along the sequence; each document has 1 to 512 tokens and one has exactly that many.
All inputs are finite; a program needn't handle non-finite values.
Results may differ from the reference program's by a relative error of at most 0.035.
Values may be sent and summed in bfloat16 or wider, within the bound.
No kernel may reach another device: no remote copies, remote signals or barrier semaphores. Data moves between devices by JAX's collectives and lax.ppermute only.
A program may use at most 128 MiB of HBM per device.

```python
import math
import jax
import jax.numpy as jnp
import numpy as np
from jax import lax

QH = 64
KVH = 8
HD = 128
SPACE_HEADS = 256
P_SIZE = 64
N = 256
TOK_DEV = 128
PACKED_TOKENS = 1024


def drawn_pair(key):
    base = jax.random.fold_in(key, 7301)
    query_seed, key_seed = jax.random.split(base, 2)
    query_cols = QH * HD
    key_cols = KVH * HD
    query_raw = jnp.clip(jax.random.normal(query_seed, (PACKED_TOKENS, query_cols), jnp.float32), -4.0, 4.0)
    key_raw = jnp.clip(jax.random.normal(key_seed, (PACKED_TOKENS, key_cols), jnp.float32), -4.0, 4.0)
    return (query_raw, key_raw)


def draw_queries(key, part):
    return drawn_pair(key)[0].astype(jnp.bfloat16)


def draw_keys_in(key, part):
    return drawn_pair(key)[1].astype(jnp.bfloat16)


def draw_log_decay(key, part):
    base = jax.random.fold_in(key, 4409)
    random_seeds = jax.random.split(base, 7)
    fast_share = 0.5
    fast_heads = jax.random.uniform(random_seeds[0], (SPACE_HEADS,), jnp.float32) < fast_share
    fast_rate = jnp.exp(jax.random.uniform(random_seeds[1], (SPACE_HEADS,), jnp.float32, math.log(1.0 / 50.0), math.log(1.0 / 30.0)))
    slow_rate = jnp.exp(jax.random.uniform(random_seeds[2], (SPACE_HEADS,), jnp.float32, math.log(0.15), math.log(0.45))) / PACKED_TOKENS
    arrival_rate = jnp.where(fast_heads, fast_rate, slow_rate)
    device_multiplier = jnp.exp(jax.random.uniform(random_seeds[3], (PACKED_TOKENS // TOK_DEV, SPACE_HEADS), jnp.float32, math.log(0.7), math.log(1.4)))
    device_multiplier = jnp.repeat(device_multiplier, TOK_DEV, axis=0)
    token_multiplier = jax.random.uniform(random_seeds[4], (PACKED_TOKENS, SPACE_HEADS), jnp.float32, 0.7, 1.4)
    spurt_rows = jax.random.randint(random_seeds[5], (2, SPACE_HEADS), 1, PACKED_TOKENS)
    spurt_length = jnp.exp(jax.random.uniform(random_seeds[6], (2, SPACE_HEADS), jnp.float32, math.log(0.22), math.log(0.6)))
    matched_flag = (jnp.arange(PACKED_TOKENS)[:, None, None] == spurt_rows[None, :, :]).astype(jnp.float32)
    spurt_count = jnp.sum(matched_flag * spurt_length[None, :, :], axis=1)
    return -(arrival_rate[None, :] * device_multiplier * token_multiplier) - spurt_count


def steps_of(rng, extent, shards, least, top_value):
    def one(axis_at, parts):
        steps = jax.random.uniform(jax.random.fold_in(jax.random.fold_in(rng, 6), axis_at), (parts,), jnp.float32, least / len(shards), top_value / len(shards))
        return jnp.repeat(jnp.exp(steps), extent[axis_at] // parts).reshape((-1,) + (1,) * (len(extent) - axis_at - 1))

    gain = one(*shards[0])
    for cut in shards[1:]:
        gain = gain * one(*cut)
    return gain


def split_up(count, total, limit, lean):
    loads = [(1 << 20) // math.isqrt(rank ** lean) + 1 for rank in range(2, count + 1)]
    surplus, counts = total - limit - (count - 1), [1] * (count - 1)
    while surplus > 0:
        movable = [i for i in range(count - 1) if counts[i] < limit]
        whole, remaining = sum([loads[i] for i in movable]), surplus
        for i in movable:
            more = min(limit - counts[i], max(1, remaining * loads[i] // whole), surplus)
            counts[i] = counts[i] + more
            surplus = surplus - more
    return np.array([limit] + counts)


def ragged_sizes(rng, count, total, most, lean):
    if count == 2:
        one = jax.random.randint(rng, (), max(1, total - most), min(most, total - 1) + 1)
        return jnp.stack([one, total - one])
    lengths = jnp.asarray(split_up(count, total, most, lean), jnp.int32)
    couples = (count - 1) // 2
    source_of, sink = lengths[1:1 + 2 * couples:2], lengths[2:2 + 2 * couples:2]
    room = jnp.minimum(source_of - 1, most - sink)
    passed = jax.random.randint(jax.random.fold_in(rng, 1), (couples,), 0, 1 << 20) % (room + 1)
    lengths = lengths.at[1:1 + 2 * couples:2].set(source_of - passed).at[2:2 + 2 * couples:2].set(sink + passed)
    return lengths[jax.random.permutation(jax.random.fold_in(rng, 2), count)]


def noise(stream_key, extent, scale, most, cuts=(), kind=jnp.bfloat16):
    values = jax.random.normal(stream_key, extent, jnp.float32) * scale
    if len(cuts) > 0:
        values = steps_of(stream_key, extent, cuts, -0.22, 0.18) * values
    return jnp.clip(values, min=-most, max=most).astype(kind)


def setup_inputs(seed: int = 0) -> dict:
    splits = jax.random.split(jax.random.key(seed), 11)
    queries = draw_queries(jax.random.fold_in(splits[10], 71), 0)
    keys_in = draw_keys_in(jax.random.fold_in(splits[10], 71), 0)
    values_in = noise(splits[2], (PACKED_TOKENS, KVH * HD), 1.0, 6.0, ((0, 8), (1, 4)))
    attn_cotan = noise(splits[3], (PACKED_TOKENS, QH * HD), 1.0, 6.0, ((0, 8), (1, 4)))
    doc_ids = jnp.searchsorted(jnp.cumsum(ragged_sizes(splits[4], 6, PACKED_TOKENS, PACKED_TOKENS // 2, 0)), jnp.arange(PACKED_TOKENS), side="right").astype(jnp.int32)
    ssd_input = noise(splits[5], (PACKED_TOKENS, SPACE_HEADS * P_SIZE), 0.05, 0.29882812, ((0, 8), (1, 4)))
    state_write = noise(splits[6], (PACKED_TOKENS, N), N ** -0.5, 0.375, ((0, 8),))
    state_read = noise(splits[7], (PACKED_TOKENS, N), 1.0, 6.0, ((0, 8),))
    log_decay = draw_log_decay(jax.random.fold_in(splits[10], 71), 0)
    ssd_cotan = noise(splits[9], (PACKED_TOKENS, SPACE_HEADS * P_SIZE), 0.02, 0.119628906, ((0, 8), (1, 4)))
    return {"queries": queries, "keys_in": keys_in, "values_in": values_in, "attn_cotan": attn_cotan, "doc_ids": doc_ids, "ssd_input": ssd_input, "state_write": state_write, "state_read": state_read, "log_decay": log_decay, "ssd_cotan": ssd_cotan}


floor_score = -1.0e30
highest = lax.Precision.HIGHEST


def attention_part(queries, keys_in, values_in, attn_cotan, doc_ids):
    length = doc_ids.shape[0]
    group_size = QH // KVH
    scale = HD ** -0.5
    positions = jnp.arange(length, dtype=jnp.int32)
    allowed = (positions[None, :] <= positions[:, None]) & (doc_ids[None, :] == doc_ids[:, None])

    def one_head(head_index):
        kv_index = head_index // group_size
        query_head = lax.dynamic_slice_in_dim(queries, head_index * HD, HD, 1)
        key_head = lax.dynamic_slice_in_dim(keys_in, kv_index * HD, HD, 1)
        value_head = lax.dynamic_slice_in_dim(values_in, kv_index * HD, HD, 1)
        cotan_head = lax.dynamic_slice_in_dim(attn_cotan, head_index * HD, HD, 1)
        scores = jnp.dot(query_head, key_head.T, preferred_element_type=jnp.float32) * scale
        row_top = jnp.max(jnp.where(allowed, scores, floor_score), axis=1)
        weights = jnp.where(allowed, jnp.exp(scores - row_top[:, None]), 0.0)
        row_total = jnp.sum(weights, axis=1)
        attn_head = (jnp.dot(weights.astype(jnp.bfloat16), value_head, preferred_element_type=jnp.float32) / row_total[:, None]).astype(jnp.bfloat16)
        log_total = row_top + jnp.log(row_total)
        row_inner = jnp.sum(cotan_head.astype(jnp.float32) * attn_head.astype(jnp.float32), axis=1)
        attn_prob = jnp.where(allowed, jnp.exp(scores - log_total[:, None]), 0.0)
        prob_grad = jnp.dot(cotan_head, value_head.T, preferred_element_type=jnp.float32)
        dscore = (attn_prob * (prob_grad - row_inner[:, None])).astype(jnp.bfloat16)
        grad_query = (jnp.dot(dscore, key_head, preferred_element_type=jnp.float32) * scale).astype(jnp.bfloat16)
        grad_key = jnp.dot(dscore.T, query_head, preferred_element_type=jnp.float32) * scale
        grad_value = jnp.dot(attn_prob.astype(jnp.bfloat16).T, cotan_head, preferred_element_type=jnp.float32)
        return attn_head, grad_query, grad_key, grad_value

    heads_out, grads_q, grads_k, grads_v = lax.map(one_head, jnp.arange(QH, dtype=jnp.int32))
    attn_out = heads_out.transpose(1, 0, 2).reshape(length, QH * HD)
    grad_q = grads_q.transpose(1, 0, 2).reshape(length, QH * HD)
    grad_k = grads_k.reshape(KVH, group_size, length, HD).sum(axis=1).astype(jnp.bfloat16)
    grad_k = grad_k.transpose(1, 0, 2).reshape(length, KVH * HD)
    grad_v = grads_v.reshape(KVH, group_size, length, HD).sum(axis=1).astype(jnp.bfloat16)
    grad_v = grad_v.transpose(1, 0, 2).reshape(length, KVH * HD)
    return attn_out, grad_q, grad_k, grad_v


def ssd_part(ssd_input, state_write, state_read, log_decay, ssd_cotan, doc_ids):
    length = doc_ids.shape[0]
    input_wide = ssd_input.astype(jnp.float32).reshape(length, SPACE_HEADS, P_SIZE)
    cotan_wide = ssd_cotan.astype(jnp.float32).reshape(length, SPACE_HEADS, P_SIZE)
    write_wide = state_write.astype(jnp.float32)
    read_wide = state_read.astype(jnp.float32)
    same_doc = jnp.concatenate([jnp.zeros((1,), dtype=bool), doc_ids[1:] == doc_ids[:-1]])
    factor = jnp.where(same_doc[:, None], jnp.exp(log_decay), 0.0)

    def forward(carried, step_inputs):
        step_factor, input_row, write_row, read_row, cotan_row = step_inputs
        carried = step_factor[:, None, None] * carried + input_row[:, :, None] * write_row[None, None, :]
        output_row = jnp.einsum("hpn,n->hp", carried, read_row, precision=highest)
        read_grad = jnp.einsum("hpn,hp->n", carried, cotan_row, precision=highest)
        return carried, (output_row, read_grad)

    empty_state = jnp.zeros((SPACE_HEADS, P_SIZE, N), jnp.float32)
    _, (outputs, grad_c) = lax.scan(forward, empty_state, (factor, input_wide, write_wide, read_wide, cotan_wide))
    next_factor = jnp.concatenate([factor[1:], jnp.zeros((1, SPACE_HEADS), jnp.float32)], axis=0)

    def backward(carried, step_inputs):
        step_factor, input_row, write_row, read_row, cotan_row = step_inputs
        carried = step_factor[:, None, None] * carried + cotan_row[:, :, None] * read_row[None, None, :]
        input_grad = jnp.einsum("hpn,n->hp", carried, write_row, precision=highest)
        write_grad = jnp.einsum("hpn,hp->n", carried, input_row, precision=highest)
        return carried, (input_grad, write_grad)

    _, (grad_x, grad_b) = lax.scan(backward, empty_state, (next_factor, input_wide, write_wide, read_wide, cotan_wide), reverse=True)
    ssd_out = outputs.reshape(length, SPACE_HEADS * P_SIZE).astype(jnp.bfloat16)
    grad_x = grad_x.reshape(length, SPACE_HEADS * P_SIZE).astype(jnp.bfloat16)
    return ssd_out, grad_x, grad_b.astype(jnp.bfloat16), grad_c.astype(jnp.bfloat16)


def reference(queries, keys_in, values_in, attn_cotan, doc_ids, ssd_input, state_write, state_read, log_decay, ssd_cotan):
    attn_out, grad_q, grad_k, grad_v = attention_part(queries, keys_in, values_in, attn_cotan, doc_ids)
    ssd_out, grad_x, grad_b, grad_c = ssd_part(ssd_input, state_write, state_read, log_decay, ssd_cotan, doc_ids)
    return (attn_out, ssd_out, grad_q, grad_k, grad_v, grad_x, grad_b, grad_c)
```

```python
import jax
import jax.numpy as jnp
from jax import lax
from jax.experimental import pallas as pl
from jax.experimental.pallas import tpu as pltpu
from jax.sharding import PartitionSpec as P

HD = 128
P_SIZE = 64
N = 256
AUX = 16
GROUP = 8
WIDTH = GROUP * P_SIZE
FLOOR = -1e30
F32 = jnp.float32
BF16 = jnp.bfloat16
highest = lax.Precision.HIGHEST
BRIEF = pl.CostEstimate(flops=1, bytes_accessed=1, transcendentals=0)


SCALAR = pl.BlockSpec(memory_space=pltpu.SMEM)
WHOLE = pl.BlockSpec(memory_space=pltpu.VMEM)
ANYWHERE = pl.BlockSpec(memory_space=pl.ANY)


def dot(a, b):
    return jnp.dot(a, b, preferred_element_type=F32)


def dot_nt(a, b):
    return lax.dot_general(a, b, (((1,), (1,)), ((), ())), preferred_element_type=F32)


def flip(a):
    return a.astype(F32).T.astype(BF16)


def running_decay(ld):
    rows = ld.shape[1]
    upper = lax.broadcasted_iota(jnp.int32, (rows, rows), 0) <= lax.broadcasted_iota(
        jnp.int32, (rows, rows), 1
    )
    return jnp.dot(ld, upper.astype(F32), preferred_element_type=F32, precision=highest)


def doc_row_col(doc_ref):
    row = doc_ref[...].astype(F32) + 1.0
    rows = row.shape[1]
    grid = jnp.broadcast_to(row, (rows, rows))
    return row, grid.T


def split(value):
    high = value.astype(BF16)
    return high, (value - high.astype(F32)).astype(BF16)


def spread(heads, first_head):
    row = lax.broadcasted_iota(jnp.int32, (heads, WIDTH), 0)
    col = lax.broadcasted_iota(jnp.int32, (heads, WIDTH), 1)
    return (lax.shift_right_logical(col, 6) + first_head == row).astype(F32).astype(BF16)


def params(mib):
    return pltpu.CompilerParams(vmem_limit_bytes=mib * 1024 * 1024)


def aux_block(decay, leaving, far):
    high, low = split(decay)
    place = lax.broadcasted_iota(jnp.int32, (AUX, decay.shape[1]), 0)
    wide = jnp.where(place == 0, high.astype(F32), low.astype(F32))
    return jnp.where(
        place < 2, wide, jnp.where(place == 2, leaving, jnp.where(place == 3, far, 0.0))
    ).astype(BF16)


def aux_rows(part):
    part = part.astype(F32)
    return part[0:1] + part[1:2], part[2:3], part[3:4]


def states_kernel(kind, x, dy, b, c, ld, doc, *refs):
    keys, values, out, packet = refs[:4] if len(refs) > 6 else (None, None, refs[0], None)
    z_in, side, ld_in, doc_in, sems = refs[-5:]
    heads = ld.shape[0]
    cols = out.shape[1]
    forward = kind[0] == 0
    part = min(cols, 2 * WIDTH)

    def copies(z, matrix):
        yield pltpu.make_async_copy(matrix, side, sems.at[2])
        for k in range(cols // part):
            to = pl.ds(k * part, part)
            source = z.at[:, pl.ds(k * part, part)]
            yield pltpu.make_async_copy(source, z_in.at[:, to], sems.at[3 + k])

    small = [
        pltpu.make_async_copy(ld, ld_in, sems.at[0]),
        pltpu.make_async_copy(doc, doc_in, sems.at[1]),
    ]
    for copy in small:
        copy.start()
    if packet is not None:
        rows, width = keys.shape
        moves = [
            pltpu.make_async_copy(part, packet.at[pl.ds(0, rows), pl.ds(k * width, width)], sem)
            for k, (part, sem) in enumerate(((keys, sems.at[sems.shape[0] - 2]), (values, sems.at[sems.shape[0] - 1])))
        ]
        for copy in moves:
            copy.start()

    @pl.when(forward)
    def _():
        for copy in copies(x, b):
            copy.start()

    @pl.when(jnp.logical_not(forward))
    def _():
        for copy in copies(dy, c):
            copy.start()

    large = list(copies(x, b))
    for copy in small:
        copy.wait()
    row, col = doc_row_col(doc_in)
    first = jnp.min(row, axis=1, keepdims=True)
    last = jnp.max(row, axis=1, keepdims=True)
    leaving, far = jnp.where(forward, last, first), jnp.where(forward, first, last)
    cum = running_decay(ld_in[...]).T
    end = cum[-1:, :]
    gap = jnp.where(forward, end - cum, cum)
    weight = jnp.where(col[:, :heads] == leaving, jnp.exp(gap), 0.0).astype(BF16)
    high, low = split(jnp.exp(jnp.broadcast_to(end, (8, heads))))
    large[0].wait()
    turned = flip(side[...])
    for t in range(cols // WIDTH):
        if t * WIDTH % part == 0:
            large[1 + t * WIDTH // part].wait()
        at = slice(t * WIDTH, (t + 1) * WIDTH)
        e = spread(heads, t * GROUP)
        z = (z_in[:, at].astype(F32) * dot(weight, e)).astype(BF16)
        out[:N, at] = dot(turned, z).astype(BF16)
        decay = dot(high, e) + dot(low, e)
        out[N:, at] = aux_block(decay[0:1], leaving, far)
    if packet is not None:
        for copy in moves:
            copy.wait()
        docs = jnp.concatenate([row] * (2 * width // rows), axis=1)
        packet[rows:, :] = jnp.broadcast_to(docs, (AUX, 2 * width)).astype(BF16)


def states(kind, x, dy, b, c, ld, doc, kv=()):
    rows, cols = x.shape
    heads = ld.shape[0]
    hbm = pl.BlockSpec(memory_space=pltpu.HBM)
    whole = lambda a: pl.BlockSpec(a.shape, lambda j, s: (0,) * a.ndim)
    shapes = [jax.ShapeDtypeStruct((N + AUX, cols), BF16)]
    if kv:
        shapes.append(jax.ShapeDtypeStruct((rows + AUX, 2 * kv[0].shape[1]), BF16))

    return pl.pallas_call(
        states_kernel,
        grid_spec=pltpu.PrefetchScalarGridSpec(
            num_scalar_prefetch=1,
            grid=(1,),
            in_specs=[hbm] * (6 + len(kv)),
            out_specs=[whole(a) for a in shapes],
            scratch_shapes=[
                pltpu.VMEM((rows, cols), BF16),
                pltpu.VMEM((rows, N), BF16),
                pltpu.VMEM((heads, rows), F32),
                pltpu.VMEM((1, rows), jnp.int32),
                pltpu.SemaphoreType.DMA((5 + max(1, cols // (2 * WIDTH)),)),
            ],
        ),
        out_shape=shapes,
        compiler_params=params(10),
        cost_estimate=BRIEF,
        name="chunk_states",
    )(kind, x, dy, b, c, ld, doc, *kv)


def merge_kernel(mine, got, out, low):
    cols = out.shape[2]
    for t in range(2 * cols // WIDTH):
        at = slice(t * WIDTH, (t + 1) * WIDTH)
        half, first = t * WIDTH // cols, t * WIDTH // cols * cols
        to = slice(t * WIDTH - first, (t + 1) * WIDTH - first)
        decay, leaving, far = aux_rows(mine[N:, at])
        decay_got, leaving_got, far_got = aux_rows(got[N:, at])
        linked = (leaving_got == far_got) & (leaving == far_got)
        total = jnp.where(linked, decay_got, 0.0) * mine[:N, at].astype(F32)
        total = (got[:N, at].astype(F32) + total).astype(BF16)
        aux = aux_block(decay * decay_got, leaving_got, far)
        out[half, :N, to] = total
        out[half, N:, to] = aux
        if half == 0:
            low[:N, to] = total
            low[N:, to] = aux


def merge(mine, got):
    rows, cols = mine.shape
    return pl.pallas_call(
        merge_kernel,
        out_shape=[
            jax.ShapeDtypeStruct((2, rows, cols // 2), BF16),
            jax.ShapeDtypeStruct((rows, cols // 2), BF16),
        ],
        compiler_params=params(4),
        cost_estimate=BRIEF,
        name="pair_merge",
    )(mine, got)


def carry_kernel(half, mine, near, extra, *refs):
    (relay, *others), (keep, out, send, sems) = refs[:-4], refs[-4:]
    cols = keep.shape[1]
    span, copies = min(cols, 2 * WIDTH), []
    for t in range(cols // WIDTH):
        at = slice(t * WIDTH, (t + 1) * WIDTH)
        own = slice(half * cols + t * WIDTH, half * cols + (t + 1) * WIDTH)
        here = near[half, :, at].astype(F32) + extra[:, at].astype(F32)
        total, coefficient, now = here[:N], None, aux_rows(here[N:])
        entering = now[1]
        for k, part in enumerate(others):
            there = part[half, :, at].astype(F32)
            if k == 0:
                there = there + relay[half, :, at].astype(F32)
            after = aux_rows(there[N:])
            step = jnp.where((now[1] == now[2]) & (after[1] == now[2]), now[0], 0.0)
            coefficient = step if coefficient is None else coefficient * step
            total = total + coefficient * there[:N]
            now = after
        decay, leaving, far = aux_rows(mine[N:, own])
        linked = (leaving == far) & (entering == far)
        passed = mine[:N, own].astype(F32) + jnp.where(linked, decay, 0.0) * total
        keep[:N, at] = total.astype(BF16)
        keep[N:, at] = aux_block(jnp.zeros_like(decay), entering, entering)
        send[:N, at] = passed.astype(BF16)
        send[N:, at] = aux_block(jnp.zeros_like(decay), leaving, leaving)
        if (t + 1) * WIDTH % span == 0:
            n = (t + 1) * WIDTH // span - 1
            piece = (slice(None), pl.ds(n * span, span))
            copies.append(pltpu.make_async_copy(send.at[piece], out.at[piece], sems.at[n]))
            copies[-1].start()
    for copy in copies:
        copy.wait()


def carries(half, mine, near, extra, others):
    out = pltpu.VMEM(extra.shape, BF16)

    def kernel(*refs):
        carry_kernel(half, *refs)

    return pl.pallas_call(
        kernel,
        in_specs=[WHOLE] * (3 + len(others)),
        out_specs=[WHOLE, ANYWHERE],
        out_shape=[out, jax.ShapeDtypeStruct(extra.shape, BF16)],
        scratch_shapes=[pltpu.VMEM(extra.shape, BF16), pltpu.SemaphoreType.DMA((4,))],
        compiler_params=params(6),
        cost_estimate=BRIEF,
        name="carry_states",
    )(mine, near, extra, *others)


def inside_kernel(
    x, dy, b, c, ld, doc, y, dx, acc, decays, cum_col, cum_row, gram, gram_t, veil, veil_t, total
):
    j = pl.program_id(0)
    heads, rows = ld.shape
    here = x.shape[1] // P_SIZE

    @pl.when(j == 0)
    def _():
        across_tokens = running_decay(ld[...])
        cum_row[...] = across_tokens
        cum = across_tokens.T
        for k in range(heads // here):
            cum_col[k] = cum[:, k * here : (k + 1) * here]
        row, col = doc_row_col(doc)
        decays[0] = jnp.exp(cum)
        decays[1] = jnp.exp(cum[-1:, :] - cum)
        decays[2] = col[:, :heads]
        places = [lax.broadcasted_iota(jnp.int32, (rows, rows), k) for k in range(2)]
        same = col == row
        veil[...] = jnp.where(same & (places[0] >= places[1]), 0.0, FLOOR)
        veil_t[...] = jnp.where(same & (places[0] <= places[1]), 0.0, FLOOR)
        gram[...] = dot_nt(c[...], b[...])
        gram_t[...] = dot_nt(b[...], c[...])
        total[...] = jnp.zeros_like(total)

    lane = lax.broadcasted_iota(jnp.int32, (1, 2 * P_SIZE), 1)
    left = (lane < P_SIZE).astype(F32).astype(BF16)
    right = (lane >= P_SIZE).astype(F32).astype(BF16)
    col_block = cum_col[j]
    row_block = cum_row[pl.ds(pl.multiple_of(j * here, here), here), :]
    for pair in range(here // 2):
        at = slice(pair * 2 * P_SIZE, (pair + 1) * 2 * P_SIZE)
        x_pair, y_pair = x[:, at], dy[:, at]
        x_both = jnp.concatenate([x_pair * left, x_pair * right], axis=0)
        y_both = jnp.concatenate([y_pair * left, y_pair * right], axis=0)
        inner = dot_nt(y_both, x_pair)
        mixed, turned, sums = [], [], 0.0
        for k in range(2):
            head = 2 * pair + k
            gap = col_block[:, head : head + 1] - row_block[head : head + 1, :]
            decay = jnp.exp(gap + veil[...])
            sums = sums + decay * inner[k * rows : (k + 1) * rows]
            mixed.append((decay * gram[...]).astype(BF16))
            turned.append((jnp.exp(veil_t[...] - gap) * gram_t[...]).astype(BF16))
        total[...] += sums
        y[:, at] = dot(jnp.concatenate(mixed, axis=1), x_both).astype(BF16)
        dx[:, at] = dot(jnp.concatenate(turned, axis=1), y_both).astype(BF16)

    @pl.when(j == pl.num_programs(0) - 1)
    def _():
        weighted = total[...]
        acc[0] = dot(weighted.T.astype(BF16), c[...])
        acc[1] = dot(weighted.astype(BF16), b[...])


def inside(x, dy, b, c, ld, doc):
    rows, cols = x.shape
    heads = ld.shape[0]
    span = min(cols, 4 * WIDTH)
    here = span // P_SIZE
    whole = lambda a: pl.BlockSpec(a.shape, lambda j: (0,) * a.ndim)
    block = pl.BlockSpec((rows, span), lambda j: (0, j))
    shapes = [
        jax.ShapeDtypeStruct((rows, cols), BF16),
        jax.ShapeDtypeStruct((rows, cols), BF16),
        jax.ShapeDtypeStruct((2, rows, N), F32),
        jax.ShapeDtypeStruct((3, rows, heads), F32),
    ]
    square = pltpu.VMEM((rows, rows), F32)
    return pl.pallas_call(
        inside_kernel,
        grid=(cols // span,),
        in_specs=[block, block, whole(b), whole(c), whole(ld), whole(doc)],
        out_specs=[block, block, whole(shapes[2]), whole(shapes[3])],
        out_shape=shapes,
        scratch_shapes=[
            pltpu.VMEM((heads // here, rows, here), F32),
            pltpu.VMEM((heads, rows), F32),
            *[square] * 5,
        ],
        compiler_params=params(10),
        cost_estimate=BRIEF,
        name="inside_chunk",
    )(x, dy, b, c, ld, doc)


def carried_weight(forward, carried, decays):
    doc = carried[N:, :HD].astype(F32)[2:3, 0:1]
    decay = jnp.where(forward, decays[0], decays[1])
    return jnp.where(decays[2] == doc, decay, 0.0).astype(BF16)


def sums_kernel(half, ranks, kind, side, x, dy, decays, carried, acc_in, *refs):
    heads = decays.shape[2]
    cols = carried.shape[1]
    forward = kind[0] == 0
    weight = carried_weight(forward, carried, decays)
    total = 0.0
    for t in range(cols // WIDTH):
        at = slice(t * WIDTH, (t + 1) * WIDTH)
        to = slice(half * cols + t * WIDTH, half * cols + (t + 1) * WIDTH)
        e = spread(heads, half * (heads // 2) + t * GROUP)
        z = jnp.where(forward, dy[:, to], x[:, to]).astype(F32)
        total = total + dot_nt((z * dot(weight, e)).astype(BF16), carried[:N, at])
    acc = refs[-1]
    acc[0] = acc_in[0] + jnp.where(forward, 0.0, total)
    acc[1] = acc_in[1] + jnp.where(forward, total, 0.0)
    if ranks > 1:
        divide(side, acc, *refs[:2])


def divide(side, acc, kept, away):
    rows = kept.shape[1]
    kept[...] = acc[:, pl.ds(pl.multiple_of(side[0] * rows, rows), rows), :]
    away[...] = acc[:, pl.ds(pl.multiple_of((1 - side[0]) * rows, rows), rows), :].astype(BF16)


def halves(acc):
    shape = (acc.shape[0], acc.shape[1] // 2, acc.shape[2])
    return [jax.ShapeDtypeStruct(shape, F32), jax.ShapeDtypeStruct(shape, BF16)]


def across_sums(half, kind, x, dy, decays, carried, acc, side=None):
    last = side is not None

    def kernel(*refs):
        sums_kernel(half, 2 if last else 1, *refs)

    return pl.pallas_call(
        kernel,
        in_specs=[SCALAR, SCALAR] + [WHOLE] * 5,
        out_specs=[WHOLE, WHOLE] if last else WHOLE,
        out_shape=halves(acc) if last else jax.ShapeDtypeStruct(acc.shape, F32),
        scratch_shapes=[pltpu.VMEM(acc.shape, F32)] if last else [],
        compiler_params=params(4),
        cost_estimate=BRIEF,
        name="across_sums",
    )(kind, side if last else kind, x, dy, decays, carried, acc)


def fetch_given(sources, buffer, sems):
    part = min(sources[0].shape[1], 2 * WIDTH)
    waits, place = [], 0
    for source in sources:
        for first in range(0, source.shape[1], part):
            piece = source.at[:, pl.ds(first, part)]
            target = buffer.at[:, pl.ds(place, part)]
            waits.append(pltpu.make_async_copy(piece, target, sems.at[place // part]))
            waits[-1].start()
            place += part
    return waits, part


def given_kernel(kind, side, x, dy, decays, acc_in, low, high, kept, away, acc, carried, sems):
    heads = decays.shape[2]
    forward = kind[0] == 0
    waits, part = fetch_given((low, high), carried, sems)
    total = 0.0
    for t in range(carried.shape[1] // WIDTH):
        if t * WIDTH % part == 0:
            waits[t * WIDTH // part].wait()
        if t == 0:
            weight = carried_weight(forward, carried, decays)
        at = slice(t * WIDTH, (t + 1) * WIDTH)
        z = jnp.where(forward, dy[:, at], x[:, at]).astype(F32)
        z = (z * dot(weight, spread(heads, t * GROUP))).astype(BF16)
        total = total + dot_nt(z, carried[:N, at])
    acc[0] = acc_in[0] + jnp.where(forward, 0.0, total)
    acc[1] = acc_in[1] + jnp.where(forward, total, 0.0)
    divide(side, acc, kept, away)


def given_sums(kind, side, x, dy, decays, low, high, acc):
    return pl.pallas_call(
        given_kernel,
        in_specs=[SCALAR, SCALAR] + [WHOLE] * 4 + [ANYWHERE] * 2,
        out_specs=[WHOLE, WHOLE],
        out_shape=halves(acc),
        scratch_shapes=[
            pltpu.VMEM(acc.shape, F32),
            pltpu.VMEM((low.shape[0], 2 * low.shape[1]), BF16),
            pltpu.SemaphoreType.DMA((8,)),
        ],
        compiler_params=params(8),
        cost_estimate=BRIEF,
        name="given_sums",
    )(kind, side, x, dy, decays, acc, low, high)


def fold_kernel(side, kept_in, moved, kept, away, acc):
    acc[...] = kept_in[...] + moved[...].astype(F32)
    divide(side, acc, kept, away)


def fold(side, kept, moved):
    return pl.pallas_call(
        fold_kernel,
        in_specs=[SCALAR, WHOLE, WHOLE],
        out_specs=[WHOLE, WHOLE],
        out_shape=halves(kept),
        scratch_shapes=[pltpu.VMEM(kept.shape, F32)],
        compiler_params=params(2),
        cost_estimate=BRIEF,
        name="sums_fold",
    )(side, kept, moved)


def outputs_kernel(half, wanted, core, b, c, decays, keep, source, y_in, dx_in, *refs):
    outs, (buffer, sems, given, arrivals) = refs[-4 - len(wanted) : -4], refs[-4:]
    waits, piece = fetch_given((source,), given, arrivals)
    heads = decays.shape[2]
    cols = keep.shape[1]
    lower = core[0] == 0
    part = min(cols, 2 * WIDTH)
    copies, weights = [], {}
    for t in range(cols // WIDTH):
        if t * WIDTH % piece == 0:
            waits[t * WIDTH // piece].wait()
        at = slice(t * WIDTH, (t + 1) * WIDTH)
        to = slice(half * cols + t * WIDTH, half * cols + (t + 1) * WIDTH)
        e = spread(heads, half * (heads // 2) + t * GROUP)
        for out, name in zip(outs, wanted):
            k = "yx".index(name)
            carried = (keep, given) if k == 0 else (given, keep)
            side, old, decay = ((c, y_in, decays[0]), (b, dx_in, decays[1]))[k]
            if t == 0:
                docs = [part_of[N:, :HD].astype(F32)[2:3, 0:1] for part_of in carried]
                doc = jnp.where(lower, docs[0], docs[1])
                weights[k] = jnp.where(decays[2] == doc, decay, 0.0).astype(BF16)
            state = jnp.where(lower, carried[0][:N, at], carried[1][:N, at])
            term = dot(weights[k], e) * dot(side[...], state)
            buffer[k, :, at] = (old[:, to].astype(F32) + term).astype(BF16)
            if (t + 1) * WIDTH % part == 0:
                n = (t + 1) * WIDTH // part - 1
                source_part = buffer.at[k, :, pl.ds(n * part, part)]
                target = out.at[:, pl.ds(half * cols + n * part, part)]
                copies.append(pltpu.make_async_copy(source_part, target, sems.at[k, n]))
                copies[-1].start()
    for copy in copies:
        copy.wait()


def across_outputs(half, wanted, core, b, c, decays, keep, given, y, dx, done=()):
    rows, cols = y.shape
    parts = max(1, cols // 2 // (2 * WIDTH))
    anywhere = pl.BlockSpec(memory_space=pl.ANY)

    def kernel(*refs):
        outputs_kernel(half, wanted, *refs)

    return pl.pallas_call(
        kernel,
        in_specs=[SCALAR] + [WHOLE] * 4 + [ANYWHERE] + [WHOLE] * 2 + [anywhere for _ in done],
        out_specs=[anywhere for _ in wanted],
        out_shape=[jax.ShapeDtypeStruct(y.shape, BF16) for _ in wanted],
        scratch_shapes=[
            pltpu.VMEM((2, rows, cols // 2), BF16),
            pltpu.SemaphoreType.DMA((2, parts)),
            pltpu.VMEM(given.shape, BF16),
            pltpu.SemaphoreType.DMA((4,)),
        ],
        input_output_aliases={8 + k: k for k in range(len(done))},
        compiler_params=params(8),
        cost_estimate=BRIEF,
        name="across_outputs",
    )(core, b, c, decays, keep, given, y, dx, *done)


def partner_kernel(other, upper, *refs):
    parts, out = refs[:-1], refs[-1]
    out[...] = (
        sum(part[pl.ds(other[0], 1)][0].astype(F32) for part in parts) + upper[...].astype(F32)
    ).astype(BF16)


def partner_part(other, upper, parts):
    return pl.pallas_call(
        partner_kernel,
        in_specs=[SCALAR] + [WHOLE] * (1 + len(parts)),
        out_specs=WHOLE,
        out_shape=jax.ShapeDtypeStruct(upper.shape, BF16),
        compiler_params=params(2),
        cost_estimate=BRIEF,
        name="partner_part",
    )(other, upper, *parts)


def finish_kernel(core, own, swapped, kept, moved, *refs):
    parts, (grad_k, grad_v, grad_b, grad_c) = refs[:-4], refs[-4:]
    cols = grad_k.shape[1]
    total = own[...] + swapped[...].astype(F32)
    total = total + sum(part[pl.ds(core[0], 1)][0].astype(F32) for part in parts)
    grad_k[...] = total[:, :cols].astype(BF16)
    grad_v[...] = total[:, cols:].astype(BF16)
    grad_b[...] = (kept[0] + moved[0].astype(F32)).astype(BF16)
    grad_c[...] = (kept[1] + moved[1].astype(F32)).astype(BF16)


def finish(core, own, swapped, kept, moved, parts):
    rows, cols = own.shape
    key = jax.ShapeDtypeStruct((rows, cols // 2), BF16)
    shared = jax.ShapeDtypeStruct(kept.shape[1:], BF16)
    return pl.pallas_call(
        finish_kernel,
        in_specs=[SCALAR] + [WHOLE] * (4 + len(parts)),
        out_shape=[key, key, shared, shared],
        compiler_params=params(2),
        cost_estimate=BRIEF,
        name="last_sums",
    )(core, own, swapped, kept, moved, *parts)


def key_blocks(lower, packet, partner, far, other, reach):
    blocks = [packet[...]]
    for k in range(1, reach + 1):
        if k % 2 == 0:
            blocks.append(far[k // 2 - 1][...])
        else:
            up = partner if k == 1 else other[k // 2 - 1]
            blocks.append(jnp.where(lower, other[k // 2][...], up[...]))
    return blocks


def attention_kernel(reach, group, kv_local, core, q, do, doc, packet, partner, *refs):
    count = len(refs) - 6 - 5
    far, other = refs[: count // 2], refs[count // 2 : count]
    o, dq, own, hold, send, upper = refs[count : count + 6]
    keys, values, veil, probs, grads = refs[count + 6 :]
    lower = core[0] == 0
    rows = q.shape[0]
    scale = HD ** (-0.5)
    row, _ = doc_row_col(doc)
    packets = key_blocks(lower, packet, partner, far, other, reach)
    for k, block in enumerate(packets):
        at = slice(k * rows, (k + 1) * rows)
        key_row = block[rows:, :HD].astype(F32)[0:1, :]
        seen = jnp.broadcast_to(key_row, (rows, rows)).T == row
        if k == 0:
            seen = seen & (
                lax.broadcasted_iota(jnp.int32, (rows, rows), 0)
                <= lax.broadcasted_iota(jnp.int32, (rows, rows), 1)
            )
        veil[at, :] = jnp.where(seen, 0.0, FLOOR)
        for g in range(kv_local):
            keys[g, at, :] = block[:rows, g * HD : (g + 1) * HD]
            values[g, at, :] = block[:rows, (kv_local + g) * HD : (kv_local + g + 1) * HD]
    for g in range(kv_local):
        k_all, v_all = keys[g], values[g]
        k_turned, v_turned = flip(k_all), flip(v_all)
        dk = dv = 0.0
        for h in range(0, group, 2):
            ats = [slice((g * group + h + i) * HD, (g * group + h + i + 1) * HD) for i in range(2)]
            q_two = jnp.concatenate([q[:, at] for at in ats], axis=0)
            do_two = jnp.concatenate([do[:, at] for at in ats], axis=0)
            do_turned = do_two.astype(F32).T
            mask = jnp.concatenate([veil[...]] * 2, axis=1)
            scores = dot(k_all, flip(q_two)) * scale + mask
            top = jnp.max(scores, axis=0, keepdims=True)
            weights = jnp.exp(scores - top)
            over = 1.0 / jnp.sum(weights, axis=0, keepdims=True)
            out = (dot(v_turned, weights.astype(BF16)) * over).astype(BF16).astype(F32)
            inner = jnp.sum(do_turned * out, axis=0, keepdims=True)
            prob = weights * over
            prob_grad = dot(v_all, do_turned.astype(BF16))
            dscore = (prob * (prob_grad - inner)).astype(BF16)
            probs[...] = prob.astype(BF16)
            grads[...] = dscore
            dq_turned = dot(k_turned, dscore) * scale
            for i, at in enumerate(ats):
                o[:, at] = out[:, i * rows : (i + 1) * rows].T.astype(BF16)
                dq[:, at] = dq_turned[:, i * rows : (i + 1) * rows].T.astype(BF16)
            dk = dk + dot(grads[...], q_two)
            dv = dv + dot(probs[...], do_two)
        for part, col in ((dk * scale, g), (dv, kv_local + g)):
            cols = slice(col * HD, (col + 1) * HD)
            own[:, cols] = part[:rows]

            def of(k):
                return part[k * rows : (k + 1) * rows] if k <= reach else jnp.zeros((rows, HD), F32)

            upper[:, cols] = jnp.where(lower, 0.0, of(1)).astype(BF16)
            for m in range(reach // 4):
                odd, even = 2 * m + 1, 2 * m + 2
                for place in range(2):
                    low_odd, up_odd = of(2 * odd - place), of(2 * odd + 1 - place)
                    low_even, up_even = of(2 * even - place), of(2 * even + 1 - place)
                    hold[m, place, :, cols] = jnp.where(lower, low_odd, up_even).astype(BF16)
                    send[m, place, :, cols] = jnp.where(lower, low_even, up_odd).astype(BF16)


def attention(core, q, do, doc, packet, partner, far, other, reach):
    rows, cols = q.shape
    kv_cols = packet.shape[1]
    kv_local = kv_cols // (2 * HD)
    group = cols // (kv_local * HD)
    blocks = reach + 1
    args = (q, do, doc, packet, partner, *far, *other)

    def kernel(*refs):
        attention_kernel(reach, group, kv_local, *refs)

    whole = lambda a: pl.BlockSpec(a.shape, lambda j, s: (0,) * a.ndim)
    shapes = [
        jax.ShapeDtypeStruct((rows, cols), BF16),
        jax.ShapeDtypeStruct((rows, cols), BF16),
        jax.ShapeDtypeStruct((rows, kv_cols), F32),
        jax.ShapeDtypeStruct((reach // 4, 2, rows, kv_cols), BF16),
        jax.ShapeDtypeStruct((reach // 4, 2, rows, kv_cols), BF16),
        jax.ShapeDtypeStruct((rows, kv_cols), BF16),
    ]
    return pl.pallas_call(
        kernel,
        grid_spec=pltpu.PrefetchScalarGridSpec(
            num_scalar_prefetch=1,
            grid=(1,),
            in_specs=[whole(a) for a in args],
            out_specs=[whole(a) for a in shapes],
            scratch_shapes=[
                pltpu.VMEM((kv_local, blocks * rows, HD), BF16),
                pltpu.VMEM((kv_local, blocks * rows, HD), BF16),
                pltpu.VMEM((blocks * rows, rows), F32),
                pltpu.VMEM((blocks * rows, 2 * rows), BF16),
                pltpu.VMEM((blocks * rows, 2 * rows), BF16),
            ],
        ),
        out_shape=shapes,
        compiler_params=params(14),
        cost_estimate=BRIEF,
        name="packed_attention",
    )(core, *args)


def shift(x, axis, by):
    count = lax.axis_size(axis)
    hops = [(i, i + by) for i in range(count) if 0 <= i + by < count]
    return lax.ppermute(x, axis, hops)


def swap(x):
    count = lax.axis_size("ctx")
    return lax.ppermute(x, "ctx", [(i, i ^ 1) for i in range(count)])


def onward(x, route):
    pairs = lax.axis_size("ctx") // 2
    hops = [(2 * p + c, 2 * route(p, c) + c) for p in range(pairs) for c in range(2)]
    return lax.ppermute(x, "ctx", [(i, k) for i, k in hops if 0 <= k < 2 * pairs])


NOWHERE = -1


def ahead(by):
    return lambda p, c: p + by * (1 - 2 * c)


def ahead_in_row(p, c):
    return ahead(1)(p, c) if p % 2 == c else NOWHERE


def ahead_to_relay(p, c):
    return ahead(2)(p, c) if p % 2 != c else NOWHERE


def ahead_direct(p, c):
    return ahead(2)(p, c) if p % 2 == c else NOWHERE


def ahead_across(p, c):
    return ahead(1)(p, c) if p % 2 != c else NOWHERE


def ahead_by_relay(pairs):
    def route(p, c):
        source = p - 2 * (1 - 2 * c)
        relayed = p % 2 != c and 0 <= source < pairs
        return p - (1 - 2 * c) if relayed else NOWHERE

    return route


def body(
    queries,
    keys_in,
    values_in,
    attn_cotan,
    doc_ids,
    ssd_input,
    state_write,
    state_read,
    log_decay,
    ssd_cotan,
):
    rows = doc_ids.shape[0]
    kv_cols = keys_in.shape[1]
    devices = lax.axis_size("ctx")
    pairs = devices // 2
    hops = pairs // 2
    reach = 2 * hops
    doc = doc_ids.reshape(1, rows)
    core = lax.rem(lax.axis_index("ctx"), 2).astype(jnp.int32).reshape(1)
    other = 1 - core

    args = (ssd_input, ssd_cotan, state_write, state_read, log_decay.T, doc)
    pinned = [pltpu.with_memory_space_constraint(a, pltpu.HBM) for a in args]
    kv = [pltpu.with_memory_space_constraint(a, pltpu.HBM) for a in (keys_in, values_in)]
    sent, packet = states(other, *pinned, kv=kv)
    got = swap(sent)
    (mine,) = states(core, *pinned)
    far = [shift(packet, "ctx", 2 * k) for k in range(1, hops + 1)]
    far, mine = lax.optimization_barrier((far, mine))
    pair, low = merge(mine, got)
    near = onward(pair, ahead_in_row)
    to_relay = onward(pair, ahead_to_relay)
    others = [onward(pair, ahead_direct)]
    others += [onward(pair, ahead(k)) for k in range(3, hops + 1)]
    partner = swap(packet)
    far_other = [swap(part) for part in far]

    _, doc_then = lax.optimization_barrier((pair, doc))
    y, dx, acc, decays = inside(*args[:5], doc_then)
    _, core_then = lax.optimization_barrier((acc, core))
    attn_out, grad_q, own, hold, send, upper = attention(
        core_then, queries, attn_cotan, doc, packet, partner, far, far_other, reach
    )
    low, own = lax.optimization_barrier((low, own))
    straight = onward(low, ahead_across)
    relayed = onward(to_relay[1], ahead_by_relay(pairs))
    hold = (hold.astype(F32) + swap(send).astype(F32)).astype(BF16)

    mine, near, straight, relayed, to_relay, others, acc, hold = lax.optimization_barrier(
        (mine, near, straight, relayed, to_relay, others, acc, hold)
    )
    others = [to_relay, *others]
    back = [onward(hold[m], lambda p, c: p - (2 * m + 1 + c)) for m in range(hops // 2)]
    keep_low, give_low = carries(0, mine, near, straight, others)
    keep, give = carries(1, mine, near, relayed, others)
    given_low, given = swap(give_low), swap(give)
    acc = across_sums(0, core, ssd_input, ssd_cotan, decays, keep_low, acc)
    acc = across_sums(1, core, ssd_input, ssd_cotan, decays, keep, acc)

    def outputs(half, after, keep, given, done=()):
        _, core_then = lax.optimization_barrier((after, core))
        return across_outputs(
            half, "yx", core_then, state_write, state_read, decays, keep, given, y, dx, done
        )

    position = lax.axis_index("head").astype(jnp.int32)
    ranks = lax.axis_size("head")

    def side_at(step):
        return lax.rem(position // step, 2).reshape(1)

    step = ranks // 2
    kept, away = given_sums(
        other, side_at(step), ssd_input, ssd_cotan, decays, given_low, given, acc
    )
    done = ()
    for half in range(ranks.bit_length() - 1):
        moved = lax.ppermute(away, "head", [(i, i ^ step) for i in range(ranks)])
        if half < 2:
            states_of = ((keep_low, given_low), (keep, given))[half]
            done = outputs(half, kept, *states_of, done)
            moved, done, back = lax.optimization_barrier((moved, done, back))
            if half == 0:
                swapped = swap(partner_part(other, upper, back))
            else:
                moved, done, swapped = lax.optimization_barrier((moved, done, swapped))
        step //= 2
        if step:
            kept, away = fold(side_at(step), kept, moved)

    grads = finish(core, own, swapped, kept, moved, back)
    return (attn_out, done[0], grad_q, grads[0], grads[1], done[1], grads[2], grads[3])


def solution(mesh):
    tokens = P("ctx", "head")
    shared = P("ctx", None)
    in_specs = (
        tokens,
        tokens,
        tokens,
        tokens,
        P("ctx"),
        tokens,
        shared,
        shared,
        tokens,
        tokens,
    )
    out_specs = (tokens,) * 6 + (P(("ctx", "head"), None),) * 2
    return jax.shard_map(body, mesh=mesh, in_specs=in_specs, out_specs=out_specs, check_vma=False)
```

```python
import jax
import jax.numpy as jnp
from jax import lax
from jax.experimental import pallas as pl
from jax.experimental.pallas import tpu as pltpu
from jax.sharding import PartitionSpec as P

HD = 128
P_SIZE = 64
N = 256
AUX = 16
GROUP = 8
WIDTH = GROUP * P_SIZE
FLOOR = -1e30
F32 = jnp.float32
BF16 = jnp.bfloat16
highest = lax.Precision.HIGHEST
BRIEF = pl.CostEstimate(flops=1, bytes_accessed=1, transcendentals=0)


SCALAR = pl.BlockSpec(memory_space=pltpu.SMEM)
WHOLE = pl.BlockSpec(memory_space=pltpu.VMEM)
ANYWHERE = pl.BlockSpec(memory_space=pl.ANY)


def dot(a, b):
    return jnp.dot(a, b, preferred_element_type=F32)


def dot_nt(a, b):
    return lax.dot_general(a, b, (((1,), (1,)), ((), ())), preferred_element_type=F32)


def flip(a):
    return a.astype(F32).T.astype(BF16)


def running_decay(ld):
    rows = ld.shape[1]
    upper = lax.broadcasted_iota(jnp.int32, (rows, rows), 0) <= lax.broadcasted_iota(
        jnp.int32, (rows, rows), 1
    )
    return jnp.dot(ld, upper.astype(F32), preferred_element_type=F32, precision=highest)


def doc_row_col(doc_ref):
    row = doc_ref[...].astype(F32) + 1.0
    rows = row.shape[1]
    grid = jnp.broadcast_to(row, (rows, rows))
    return row, grid.T


def split(value):
    high = value.astype(BF16)
    return high, (value - high.astype(F32)).astype(BF16)


def spread(heads, first_head):
    row = lax.broadcasted_iota(jnp.int32, (heads, WIDTH), 0)
    col = lax.broadcasted_iota(jnp.int32, (heads, WIDTH), 1)
    return (lax.shift_right_logical(col, 6) + first_head == row).astype(F32).astype(BF16)


def params(mib):
    return pltpu.CompilerParams(vmem_limit_bytes=mib * 1024 * 1024)


def aux_block(decay, leaving, far):
    high, low = split(decay)
    place = lax.broadcasted_iota(jnp.int32, (AUX, decay.shape[1]), 0)
    wide = jnp.where(place == 0, high.astype(F32), low.astype(F32))
    return jnp.where(
        place < 2, wide, jnp.where(place == 2, leaving, jnp.where(place == 3, far, 0.0))
    ).astype(BF16)


def aux_rows(part):
    part = part.astype(F32)
    return part[0:1] + part[1:2], part[2:3], part[3:4]


def states_kernel(kind, x, dy, b, c, ld, doc, *refs):
    keys, values, out, packet = refs[:4] if len(refs) > 6 else (None, None, refs[0], None)
    z_in, side, ld_in, doc_in, sems = refs[-5:]
    heads = ld.shape[0]
    cols = out.shape[1]
    forward = kind[0] == 0
    part = min(cols, 2 * WIDTH)

    def copies(z, matrix):
        yield pltpu.make_async_copy(matrix, side, sems.at[2])
        for k in range(cols // part):
            to = pl.ds(k * part, part)
            source = z.at[:, pl.ds(k * part, part)]
            yield pltpu.make_async_copy(source, z_in.at[:, to], sems.at[3 + k])

    small = [
        pltpu.make_async_copy(ld, ld_in, sems.at[0]),
        pltpu.make_async_copy(doc, doc_in, sems.at[1]),
    ]
    for copy in small:
        copy.start()
    if packet is not None:
        rows, width = keys.shape
        moves = [
            pltpu.make_async_copy(part, packet.at[pl.ds(0, rows), pl.ds(k * width, width)], sem)
            for k, (part, sem) in enumerate(((keys, sems.at[sems.shape[0] - 2]), (values, sems.at[sems.shape[0] - 1])))
        ]
        for copy in moves:
            copy.start()

    @pl.when(forward)
    def _():
        for copy in copies(x, b):
            copy.start()

    @pl.when(jnp.logical_not(forward))
    def _():
        for copy in copies(dy, c):
            copy.start()

    large = list(copies(x, b))
    for copy in small:
        copy.wait()
    row, col = doc_row_col(doc_in)
    first = jnp.min(row, axis=1, keepdims=True)
    last = jnp.max(row, axis=1, keepdims=True)
    leaving, far = jnp.where(forward, last, first), jnp.where(forward, first, last)
    cum = running_decay(ld_in[...]).T
    end = cum[-1:, :]
    gap = jnp.where(forward, end - cum, cum)
    weight = jnp.where(col[:, :heads] == leaving, jnp.exp(gap), 0.0).astype(BF16)
    high, low = split(jnp.exp(jnp.broadcast_to(end, (8, heads))))
    large[0].wait()
    turned = flip(side[...])
    for t in range(cols // WIDTH):
        if t * WIDTH % part == 0:
            large[1 + t * WIDTH // part].wait()
        at = slice(t * WIDTH, (t + 1) * WIDTH)
        e = spread(heads, t * GROUP)
        z = (z_in[:, at].astype(F32) * dot(weight, e)).astype(BF16)
        out[:N, at] = dot(turned, z).astype(BF16)
        decay = dot(high, e) + dot(low, e)
        out[N:, at] = aux_block(decay[0:1], leaving, far)
    if packet is not None:
        for copy in moves:
            copy.wait()
        docs = jnp.concatenate([row] * (2 * width // rows), axis=1)
        packet[rows:, :] = jnp.broadcast_to(docs, (AUX, 2 * width)).astype(BF16)


def states(kind, x, dy, b, c, ld, doc, kv=()):
    rows, cols = x.shape
    heads = ld.shape[0]
    hbm = pl.BlockSpec(memory_space=pltpu.HBM)
    whole = lambda a: pl.BlockSpec(a.shape, lambda j, s: (0,) * a.ndim)
    shapes = [jax.ShapeDtypeStruct((N + AUX, cols), BF16)]
    if kv:
        shapes.append(jax.ShapeDtypeStruct((rows + AUX, 2 * kv[0].shape[1]), BF16))

    return pl.pallas_call(
        states_kernel,
        grid_spec=pltpu.PrefetchScalarGridSpec(
            num_scalar_prefetch=1,
            grid=(1,),
            in_specs=[hbm] * (6 + len(kv)),
            out_specs=[whole(a) for a in shapes],
            scratch_shapes=[
                pltpu.VMEM((rows, cols), BF16),
                pltpu.VMEM((rows, N), BF16),
                pltpu.VMEM((heads, rows), F32),
                pltpu.VMEM((1, rows), jnp.int32),
                pltpu.SemaphoreType.DMA((5 + max(1, cols // (2 * WIDTH)),)),
            ],
        ),
        out_shape=shapes,
        compiler_params=params(10),
        cost_estimate=BRIEF,
        name="chunk_states",
    )(kind, x, dy, b, c, ld, doc, *kv)


def merge_kernel(mine, got, out, low):
    cols = out.shape[2]
    for t in range(2 * cols // WIDTH):
        at = slice(t * WIDTH, (t + 1) * WIDTH)
        half, first = t * WIDTH // cols, t * WIDTH // cols * cols
        to = slice(t * WIDTH - first, (t + 1) * WIDTH - first)
        decay, leaving, far = aux_rows(mine[N:, at])
        decay_got, leaving_got, far_got = aux_rows(got[N:, at])
        linked = (leaving_got == far_got) & (leaving == far_got)
        total = jnp.where(linked, decay_got, 0.0) * mine[:N, at].astype(F32)
        total = (got[:N, at].astype(F32) + total).astype(BF16)
        aux = aux_block(decay * decay_got, leaving_got, far)
        out[half, :N, to] = total
        out[half, N:, to] = aux
        if half == 0:
            low[:N, to] = total
            low[N:, to] = aux


def merge(mine, got):
    rows, cols = mine.shape
    return pl.pallas_call(
        merge_kernel,
        out_shape=[
            jax.ShapeDtypeStruct((2, rows, cols // 2), BF16),
            jax.ShapeDtypeStruct((rows, cols // 2), BF16),
        ],
        compiler_params=params(4),
        cost_estimate=BRIEF,
        name="pair_merge",
    )(mine, got)


def carry_kernel(half, mine, near, extra, *refs):
    (relay, *others), (keep, out, send, sems) = refs[:-4], refs[-4:]
    cols = keep.shape[1]
    span, copies = min(cols, 2 * WIDTH), []
    for t in range(cols // WIDTH):
        at = slice(t * WIDTH, (t + 1) * WIDTH)
        own = slice(half * cols + t * WIDTH, half * cols + (t + 1) * WIDTH)
        here = near[half, :, at].astype(F32) + extra[:, at].astype(F32)
        total, coefficient, now = here[:N], None, aux_rows(here[N:])
        entering = now[1]
        for k, part in enumerate(others):
            there = part[half, :, at].astype(F32)
            if k == 0:
                there = there + relay[half, :, at].astype(F32)
            after = aux_rows(there[N:])
            step = jnp.where((now[1] == now[2]) & (after[1] == now[2]), now[0], 0.0)
            coefficient = step if coefficient is None else coefficient * step
            total = total + coefficient * there[:N]
            now = after
        decay, leaving, far = aux_rows(mine[N:, own])
        linked = (leaving == far) & (entering == far)
        passed = mine[:N, own].astype(F32) + jnp.where(linked, decay, 0.0) * total
        keep[:N, at] = total.astype(BF16)
        keep[N:, at] = aux_block(jnp.zeros_like(decay), entering, entering)
        send[:N, at] = passed.astype(BF16)
        send[N:, at] = aux_block(jnp.zeros_like(decay), leaving, leaving)
        if (t + 1) * WIDTH % span == 0:
            n = (t + 1) * WIDTH // span - 1
            piece = (slice(None), pl.ds(n * span, span))
            copies.append(pltpu.make_async_copy(send.at[piece], out.at[piece], sems.at[n]))
            copies[-1].start()
    for copy in copies:
        copy.wait()


def carries(half, mine, near, extra, others):
    out = pltpu.VMEM(extra.shape, BF16)

    def kernel(*refs):
        carry_kernel(half, *refs)

    return pl.pallas_call(
        kernel,
        in_specs=[WHOLE] * (3 + len(others)),
        out_specs=[WHOLE, ANYWHERE],
        out_shape=[out, jax.ShapeDtypeStruct(extra.shape, BF16)],
        scratch_shapes=[pltpu.VMEM(extra.shape, BF16), pltpu.SemaphoreType.DMA((4,))],
        compiler_params=params(6),
        cost_estimate=BRIEF,
        name="carry_states",
    )(mine, near, extra, *others)


def inside_kernel(
    x, dy, b, c, ld, doc, y, dx, acc, decays, cum_col, cum_row, gram, gram_t, veil, veil_t, total
):
    j = pl.program_id(0)
    heads, rows = ld.shape
    here = x.shape[1] // P_SIZE

    @pl.when(j == 0)
    def _():
        across_tokens = running_decay(ld[...])
        cum_row[...] = across_tokens
        cum = across_tokens.T
        for k in range(heads // here):
            cum_col[k] = cum[:, k * here : (k + 1) * here]
        row, col = doc_row_col(doc)
        decays[0] = jnp.exp(cum)
        decays[1] = jnp.exp(cum[-1:, :] - cum)
        decays[2] = col[:, :heads]
        places = [lax.broadcasted_iota(jnp.int32, (rows, rows), k) for k in range(2)]
        same = col == row
        veil[...] = jnp.where(same & (places[0] >= places[1]), 0.0, FLOOR)
        veil_t[...] = jnp.where(same & (places[0] <= places[1]), 0.0, FLOOR)
        gram[...] = dot_nt(c[...], b[...])
        gram_t[...] = dot_nt(b[...], c[...])
        total[...] = jnp.zeros_like(total)

    lane = lax.broadcasted_iota(jnp.int32, (1, 2 * P_SIZE), 1)
    left = (lane < P_SIZE).astype(F32).astype(BF16)
    right = (lane >= P_SIZE).astype(F32).astype(BF16)
    col_block = cum_col[j]
    row_block = cum_row[pl.ds(pl.multiple_of(j * here, here), here), :]
    for pair in range(here // 2):
        at = slice(pair * 2 * P_SIZE, (pair + 1) * 2 * P_SIZE)
        x_pair, y_pair = x[:, at], dy[:, at]
        x_both = jnp.concatenate([x_pair * left, x_pair * right], axis=0)
        y_both = jnp.concatenate([y_pair * left, y_pair * right], axis=0)
        inner = dot_nt(y_both, x_pair)
        mixed, turned, sums = [], [], 0.0
        for k in range(2):
            head = 2 * pair + k
            gap = col_block[:, head : head + 1] - row_block[head : head + 1, :]
            decay = jnp.exp(gap + veil[...])
            sums = sums + decay * inner[k * rows : (k + 1) * rows]
            mixed.append((decay * gram[...]).astype(BF16))
            turned.append((jnp.exp(veil_t[...] - gap) * gram_t[...]).astype(BF16))
        total[...] += sums
        y[:, at] = dot(jnp.concatenate(mixed, axis=1), x_both).astype(BF16)
        dx[:, at] = dot(jnp.concatenate(turned, axis=1), y_both).astype(BF16)

    @pl.when(j == pl.num_programs(0) - 1)
    def _():
        weighted = total[...]
        acc[0] = dot(weighted.T.astype(BF16), c[...])
        acc[1] = dot(weighted.astype(BF16), b[...])


def inside(x, dy, b, c, ld, doc):
    rows, cols = x.shape
    heads = ld.shape[0]
    span = min(cols, 4 * WIDTH)
    here = span // P_SIZE
    whole = lambda a: pl.BlockSpec(a.shape, lambda j: (0,) * a.ndim)
    block = pl.BlockSpec((rows, span), lambda j: (0, j))
    shapes = [
        jax.ShapeDtypeStruct((rows, cols), BF16),
        jax.ShapeDtypeStruct((rows, cols), BF16),
        jax.ShapeDtypeStruct((2, rows, N), F32),
        jax.ShapeDtypeStruct((3, rows, heads), F32),
    ]
    square = pltpu.VMEM((rows, rows), F32)
    return pl.pallas_call(
        inside_kernel,
        grid=(cols // span,),
        in_specs=[block, block, whole(b), whole(c), whole(ld), whole(doc)],
        out_specs=[block, block, whole(shapes[2]), whole(shapes[3])],
        out_shape=shapes,
        scratch_shapes=[
            pltpu.VMEM((heads // here, rows, here), F32),
            pltpu.VMEM((heads, rows), F32),
            *[square] * 5,
        ],
        compiler_params=params(10),
        cost_estimate=BRIEF,
        name="inside_chunk",
    )(x, dy, b, c, ld, doc)


def carried_weight(forward, carried, decays):
    doc = carried[N:, :HD].astype(F32)[2:3, 0:1]
    decay = jnp.where(forward, decays[0], decays[1])
    return jnp.where(decays[2] == doc, decay, 0.0).astype(BF16)


def begin(picked, one, two, target, sem):
    copies = [pltpu.make_async_copy(source, target, sem) for source in (one, two)]

    @pl.when(picked)
    def _():
        copies[1].start()

    @pl.when(jnp.logical_not(picked))
    def _():
        copies[0].start()

    return copies[0]


def sums_kernel(half, kind, x, dy, decays, carried, acc_in, acc, z_in, sems):
    heads = decays.shape[2]
    cols = carried.shape[1]
    part = min(cols, 2 * WIDTH)
    forward = kind[0] == 0
    waits = []
    for n in range(cols // part):
        source = [a.at[:, pl.ds(half * cols + n * part, part)] for a in (x, dy)]
        waits.append(begin(forward, *source, z_in.at[:, pl.ds(n * part, part)], sems.at[n]))
    weight = carried_weight(forward, carried, decays)
    total = 0.0
    for t in range(cols // WIDTH):
        if t * WIDTH % part == 0:
            waits[t * WIDTH // part].wait()
        at = slice(t * WIDTH, (t + 1) * WIDTH)
        e = spread(heads, half * (heads // 2) + t * GROUP)
        z = (z_in[:, at].astype(F32) * dot(weight, e)).astype(BF16)
        total = total + dot_nt(z, carried[:N, at])
    acc[0] = acc_in[0] + jnp.where(forward, 0.0, total)
    acc[1] = acc_in[1] + jnp.where(forward, total, 0.0)


def divide(side, acc, kept, away):
    rows = kept.shape[1]
    kept[...] = acc[:, pl.ds(pl.multiple_of(side[0] * rows, rows), rows), :]
    away[...] = acc[:, pl.ds(pl.multiple_of((1 - side[0]) * rows, rows), rows), :].astype(BF16)


def halves(acc):
    shape = (acc.shape[0], acc.shape[1] // 2, acc.shape[2])
    return [jax.ShapeDtypeStruct(shape, F32), jax.ShapeDtypeStruct(shape, BF16)]


def across_sums(half, kind, x, dy, decays, carried, acc):
    def kernel(*refs):
        sums_kernel(half, *refs)

    return pl.pallas_call(
        kernel,
        in_specs=[SCALAR, ANYWHERE, ANYWHERE, WHOLE, WHOLE, WHOLE],
        out_specs=WHOLE,
        out_shape=jax.ShapeDtypeStruct(acc.shape, F32),
        scratch_shapes=[
            pltpu.VMEM((x.shape[0], carried.shape[1]), BF16),
            pltpu.SemaphoreType.DMA((4,)),
        ],
        compiler_params=params(5),
        cost_estimate=BRIEF,
        name="across_sums",
    )(kind, x, dy, decays, carried, acc)


def fetch_given(sources, buffer, sems):
    part = min(sources[0].shape[1], 2 * WIDTH)
    waits, place = [], 0
    for source in sources:
        for first in range(0, source.shape[1], part):
            piece = source.at[:, pl.ds(first, part)]
            target = buffer.at[:, pl.ds(place, part)]
            waits.append(pltpu.make_async_copy(piece, target, sems.at[place // part]))
            waits[-1].start()
            place += part
    return waits, part


def given_kernel(
    kind, side, x, dy, decays, acc_in, low, high, kept, away, acc, carried, sems, z_in, z_sems
):
    heads = decays.shape[2]
    forward = kind[0] == 0
    waits, part = fetch_given((low, high), carried, sems)
    z_waits = []
    for n in range(len(waits)):
        piece = (slice(None), pl.ds(n * part, part))
        z_waits.append(begin(forward, x.at[piece], dy.at[piece], z_in.at[piece], z_sems.at[n]))
    total = 0.0
    for t in range(carried.shape[1] // WIDTH):
        if t * WIDTH % part == 0:
            waits[t * WIDTH // part].wait()
            z_waits[t * WIDTH // part].wait()
        if t == 0:
            weight = carried_weight(forward, carried, decays)
        at = slice(t * WIDTH, (t + 1) * WIDTH)
        z = z_in[:, at].astype(F32)
        z = (z * dot(weight, spread(heads, t * GROUP))).astype(BF16)
        total = total + dot_nt(z, carried[:N, at])
    acc[0] = acc_in[0] + jnp.where(forward, 0.0, total)
    acc[1] = acc_in[1] + jnp.where(forward, total, 0.0)
    divide(side, acc, kept, away)


def given_sums(kind, side, x, dy, decays, low, high, acc):
    return pl.pallas_call(
        given_kernel,
        in_specs=[SCALAR, SCALAR, ANYWHERE, ANYWHERE, WHOLE, WHOLE, ANYWHERE, ANYWHERE],
        out_specs=[WHOLE, WHOLE],
        out_shape=halves(acc),
        scratch_shapes=[
            pltpu.VMEM(acc.shape, F32),
            pltpu.VMEM((low.shape[0], 2 * low.shape[1]), BF16),
            pltpu.SemaphoreType.DMA((8,)),
            pltpu.VMEM(x.shape, BF16),
            pltpu.SemaphoreType.DMA((8,)),
        ],
        compiler_params=params(8),
        cost_estimate=BRIEF,
        name="given_sums",
    )(kind, side, x, dy, decays, acc, low, high)


def fold_kernel(side, kept_in, moved, kept, away, acc):
    acc[...] = kept_in[...] + moved[...].astype(F32)
    divide(side, acc, kept, away)


def fold(side, kept, moved):
    return pl.pallas_call(
        fold_kernel,
        in_specs=[SCALAR, WHOLE, WHOLE],
        out_specs=[WHOLE, WHOLE],
        out_shape=halves(kept),
        scratch_shapes=[pltpu.VMEM(kept.shape, F32)],
        compiler_params=params(2),
        cost_estimate=BRIEF,
        name="sums_fold",
    )(side, kept, moved)


def outputs_kernel(half, wanted, core, b, c, decays, keep, source, y_in, dx_in, *refs):
    outs, (buffer, sems, given, arrivals) = refs[-4 - len(wanted) : -4], refs[-4:]
    waits, piece = fetch_given((source,), given, arrivals)
    heads = decays.shape[2]
    cols = keep.shape[1]
    lower = core[0] == 0
    part = min(cols, 2 * WIDTH)
    copies, weights = [], {}
    for t in range(cols // WIDTH):
        if t * WIDTH % piece == 0:
            waits[t * WIDTH // piece].wait()
        at = slice(t * WIDTH, (t + 1) * WIDTH)
        to = slice(half * cols + t * WIDTH, half * cols + (t + 1) * WIDTH)
        e = spread(heads, half * (heads // 2) + t * GROUP)
        for out, name in zip(outs, wanted):
            k = "yx".index(name)
            carried = (keep, given) if k == 0 else (given, keep)
            side, old, decay = ((c, y_in, decays[0]), (b, dx_in, decays[1]))[k]
            if t == 0:
                docs = [part_of[N:, :HD].astype(F32)[2:3, 0:1] for part_of in carried]
                doc = jnp.where(lower, docs[0], docs[1])
                weights[k] = jnp.where(decays[2] == doc, decay, 0.0).astype(BF16)
            state = jnp.where(lower, carried[0][:N, at], carried[1][:N, at])
            term = dot(weights[k], e) * dot(side[...], state)
            buffer[k, :, at] = (old[:, to].astype(F32) + term).astype(BF16)
            if (t + 1) * WIDTH % part == 0:
                n = (t + 1) * WIDTH // part - 1
                source_part = buffer.at[k, :, pl.ds(n * part, part)]
                target = out.at[:, pl.ds(half * cols + n * part, part)]
                copies.append(pltpu.make_async_copy(source_part, target, sems.at[k, n]))
                copies[-1].start()
    for copy in copies:
        copy.wait()


def across_outputs(half, wanted, core, b, c, decays, keep, given, y, dx, done=()):
    rows, cols = y.shape
    parts = max(1, cols // 2 // (2 * WIDTH))
    anywhere = pl.BlockSpec(memory_space=pl.ANY)

    def kernel(*refs):
        outputs_kernel(half, wanted, *refs)

    return pl.pallas_call(
        kernel,
        in_specs=[SCALAR] + [WHOLE] * 4 + [ANYWHERE] + [WHOLE] * 2 + [anywhere for _ in done],
        out_specs=[anywhere for _ in wanted],
        out_shape=[jax.ShapeDtypeStruct(y.shape, BF16) for _ in wanted],
        scratch_shapes=[
            pltpu.VMEM((2, rows, cols // 2), BF16),
            pltpu.SemaphoreType.DMA((2, parts)),
            pltpu.VMEM(given.shape, BF16),
            pltpu.SemaphoreType.DMA((4,)),
        ],
        input_output_aliases={8 + k: k for k in range(len(done))},
        compiler_params=params(8),
        cost_estimate=BRIEF,
        name="across_outputs",
    )(core, b, c, decays, keep, given, y, dx, *done)


def partner_kernel(other, upper, *refs):
    parts, out = refs[:-1], refs[-1]
    out[...] = (
        sum(part[pl.ds(other[0], 1)][0].astype(F32) for part in parts) + upper[...].astype(F32)
    ).astype(BF16)


def partner_part(other, upper, parts):
    return pl.pallas_call(
        partner_kernel,
        in_specs=[SCALAR] + [WHOLE] * (1 + len(parts)),
        out_specs=WHOLE,
        out_shape=jax.ShapeDtypeStruct(upper.shape, BF16),
        compiler_params=params(2),
        cost_estimate=BRIEF,
        name="partner_part",
    )(other, upper, *parts)


def finish_kernel(core, own, swapped, kept, moved, *refs):
    parts, (grad_k, grad_v, grad_b, grad_c) = refs[:-4], refs[-4:]
    cols = grad_k.shape[1]
    total = own[...] + swapped[...].astype(F32)
    total = total + sum(part[pl.ds(core[0], 1)][0].astype(F32) for part in parts)
    grad_k[...] = total[:, :cols].astype(BF16)
    grad_v[...] = total[:, cols:].astype(BF16)
    grad_b[...] = (kept[0] + moved[0].astype(F32)).astype(BF16)
    grad_c[...] = (kept[1] + moved[1].astype(F32)).astype(BF16)


def finish(core, own, swapped, kept, moved, parts):
    rows, cols = own.shape
    key = jax.ShapeDtypeStruct((rows, cols // 2), BF16)
    shared = jax.ShapeDtypeStruct(kept.shape[1:], BF16)
    return pl.pallas_call(
        finish_kernel,
        in_specs=[SCALAR] + [WHOLE] * (4 + len(parts)),
        out_shape=[key, key, shared, shared],
        compiler_params=params(2),
        cost_estimate=BRIEF,
        name="last_sums",
    )(core, own, swapped, kept, moved, *parts)


def key_blocks(lower, packet, partner, far, other, reach):
    blocks = [packet[...]]
    for k in range(1, reach + 1):
        if k % 2 == 0:
            blocks.append(far[k // 2 - 1][...])
        else:
            up = partner if k == 1 else other[k // 2 - 1]
            blocks.append(jnp.where(lower, other[k // 2][...], up[...]))
    return blocks


def attention_kernel(reach, group, kv_local, core, q, do, doc, packet, partner, *refs):
    count = len(refs) - 6 - 5
    far, other = refs[: count // 2], refs[count // 2 : count]
    o, dq, own, hold, send, upper = refs[count : count + 6]
    keys, values, veil, probs, grads = refs[count + 6 :]
    lower = core[0] == 0
    rows = q.shape[0]
    scale = HD ** (-0.5)
    row, _ = doc_row_col(doc)
    packets = key_blocks(lower, packet, partner, far, other, reach)
    for k, block in enumerate(packets):
        at = slice(k * rows, (k + 1) * rows)
        key_row = block[rows:, :HD].astype(F32)[0:1, :]
        seen = jnp.broadcast_to(key_row, (rows, rows)).T == row
        if k == 0:
            seen = seen & (
                lax.broadcasted_iota(jnp.int32, (rows, rows), 0)
                <= lax.broadcasted_iota(jnp.int32, (rows, rows), 1)
            )
        veil[at, :] = jnp.where(seen, 0.0, FLOOR)
        for g in range(kv_local):
            keys[g, at, :] = block[:rows, g * HD : (g + 1) * HD]
            values[g, at, :] = block[:rows, (kv_local + g) * HD : (kv_local + g + 1) * HD]
    for g in range(kv_local):
        k_all, v_all = keys[g], values[g]
        k_turned, v_turned = flip(k_all), flip(v_all)
        dk = dv = 0.0
        for h in range(0, group, 2):
            ats = [slice((g * group + h + i) * HD, (g * group + h + i + 1) * HD) for i in range(2)]
            q_two = jnp.concatenate([q[:, at] for at in ats], axis=0)
            do_two = jnp.concatenate([do[:, at] for at in ats], axis=0)
            do_turned = do_two.astype(F32).T
            mask = jnp.concatenate([veil[...]] * 2, axis=1)
            scores = dot(k_all, flip(q_two)) * scale + mask
            top = jnp.max(scores, axis=0, keepdims=True)
            weights = jnp.exp(scores - top)
            over = 1.0 / jnp.sum(weights, axis=0, keepdims=True)
            out = (dot(v_turned, weights.astype(BF16)) * over).astype(BF16).astype(F32)
            inner = jnp.sum(do_turned * out, axis=0, keepdims=True)
            prob = weights * over
            prob_grad = dot(v_all, do_turned.astype(BF16))
            dscore = (prob * (prob_grad - inner)).astype(BF16)
            probs[...] = prob.astype(BF16)
            grads[...] = dscore
            dq_turned = dot(k_turned, dscore) * scale
            for i, at in enumerate(ats):
                o[:, at] = out[:, i * rows : (i + 1) * rows].T.astype(BF16)
                dq[:, at] = dq_turned[:, i * rows : (i + 1) * rows].T.astype(BF16)
            dk = dk + dot(grads[...], q_two)
            dv = dv + dot(probs[...], do_two)
        for part, col in ((dk * scale, g), (dv, kv_local + g)):
            cols = slice(col * HD, (col + 1) * HD)
            own[:, cols] = part[:rows]

            def of(k):
                return part[k * rows : (k + 1) * rows] if k <= reach else jnp.zeros((rows, HD), F32)

            upper[:, cols] = jnp.where(lower, 0.0, of(1)).astype(BF16)
            for m in range(reach // 4):
                odd, even = 2 * m + 1, 2 * m + 2
                for place in range(2):
                    low_odd, up_odd = of(2 * odd - place), of(2 * odd + 1 - place)
                    low_even, up_even = of(2 * even - place), of(2 * even + 1 - place)
                    hold[m, place, :, cols] = jnp.where(lower, low_odd, up_even).astype(BF16)
                    send[m, place, :, cols] = jnp.where(lower, low_even, up_odd).astype(BF16)


def attention(core, q, do, doc, packet, partner, far, other, reach):
    rows, cols = q.shape
    kv_cols = packet.shape[1]
    kv_local = kv_cols // (2 * HD)
    group = cols // (kv_local * HD)
    blocks = reach + 1
    args = (q, do, doc, packet, partner, *far, *other)

    def kernel(*refs):
        attention_kernel(reach, group, kv_local, *refs)

    whole = lambda a: pl.BlockSpec(a.shape, lambda j, s: (0,) * a.ndim)
    shapes = [
        jax.ShapeDtypeStruct((rows, cols), BF16),
        jax.ShapeDtypeStruct((rows, cols), BF16),
        jax.ShapeDtypeStruct((rows, kv_cols), F32),
        jax.ShapeDtypeStruct((reach // 4, 2, rows, kv_cols), BF16),
        jax.ShapeDtypeStruct((reach // 4, 2, rows, kv_cols), BF16),
        jax.ShapeDtypeStruct((rows, kv_cols), BF16),
    ]
    return pl.pallas_call(
        kernel,
        grid_spec=pltpu.PrefetchScalarGridSpec(
            num_scalar_prefetch=1,
            grid=(1,),
            in_specs=[whole(a) for a in args],
            out_specs=[whole(a) for a in shapes],
            scratch_shapes=[
                pltpu.VMEM((kv_local, blocks * rows, HD), BF16),
                pltpu.VMEM((kv_local, blocks * rows, HD), BF16),
                pltpu.VMEM((blocks * rows, rows), F32),
                pltpu.VMEM((blocks * rows, 2 * rows), BF16),
                pltpu.VMEM((blocks * rows, 2 * rows), BF16),
            ],
        ),
        out_shape=shapes,
        compiler_params=params(14),
        cost_estimate=BRIEF,
        name="packed_attention",
    )(core, *args)


def shift(x, axis, by):
    count = lax.axis_size(axis)
    hops = [(i, i + by) for i in range(count) if 0 <= i + by < count]
    return lax.ppermute(x, axis, hops)


def swap(x):
    count = lax.axis_size("ctx")
    return lax.ppermute(x, "ctx", [(i, i ^ 1) for i in range(count)])


def onward(x, route):
    pairs = lax.axis_size("ctx") // 2
    hops = [(2 * p + c, 2 * route(p, c) + c) for p in range(pairs) for c in range(2)]
    return lax.ppermute(x, "ctx", [(i, k) for i, k in hops if 0 <= k < 2 * pairs])


NOWHERE = -1


def ahead(by):
    return lambda p, c: p + by * (1 - 2 * c)


def ahead_in_row(p, c):
    return ahead(1)(p, c) if p % 2 == c else NOWHERE


def ahead_to_relay(p, c):
    return ahead(2)(p, c) if p % 2 != c else NOWHERE


def ahead_direct(p, c):
    return ahead(2)(p, c) if p % 2 == c else NOWHERE


def ahead_across(p, c):
    return ahead(1)(p, c) if p % 2 != c else NOWHERE


def ahead_by_relay(pairs):
    def route(p, c):
        source = p - 2 * (1 - 2 * c)
        relayed = p % 2 != c and 0 <= source < pairs
        return p - (1 - 2 * c) if relayed else NOWHERE

    return route


def body(
    queries,
    keys_in,
    values_in,
    attn_cotan,
    doc_ids,
    ssd_input,
    state_write,
    state_read,
    log_decay,
    ssd_cotan,
):
    rows = doc_ids.shape[0]
    kv_cols = keys_in.shape[1]
    devices = lax.axis_size("ctx")
    pairs = devices // 2
    hops = pairs // 2
    reach = 2 * hops
    doc = doc_ids.reshape(1, rows)
    core = lax.rem(lax.axis_index("ctx"), 2).astype(jnp.int32).reshape(1)
    other = 1 - core

    args = (ssd_input, ssd_cotan, state_write, state_read, log_decay.T, doc)
    pinned = [pltpu.with_memory_space_constraint(a, pltpu.HBM) for a in args]
    kv = [pltpu.with_memory_space_constraint(a, pltpu.HBM) for a in (keys_in, values_in)]
    sent, packet = states(other, *pinned, kv=kv)
    got = swap(sent)
    (mine,) = states(core, *pinned)
    far = [shift(packet, "ctx", 2 * k) for k in range(1, hops + 1)]
    far, mine = lax.optimization_barrier((far, mine))
    pair, low = merge(mine, got)
    near = onward(pair, ahead_in_row)
    to_relay = onward(pair, ahead_to_relay)
    others = [onward(pair, ahead_direct)]
    others += [onward(pair, ahead(k)) for k in range(3, hops + 1)]
    partner = swap(packet)
    far_other = [swap(part) for part in far]

    _, doc_then = lax.optimization_barrier((pair, doc))
    y, dx, acc, decays = inside(*args[:5], doc_then)
    _, core_then = lax.optimization_barrier((acc, core))
    attn_out, grad_q, own, hold, send, upper = attention(
        core_then, queries, attn_cotan, doc, packet, partner, far, far_other, reach
    )
    low, own = lax.optimization_barrier((low, own))
    straight = onward(low, ahead_across)
    relayed = onward(to_relay[1], ahead_by_relay(pairs))
    near, send = lax.optimization_barrier((near, send))
    hold = (hold.astype(F32) + swap(send).astype(F32)).astype(BF16)

    mine, near, straight, relayed, to_relay, others, acc, hold = lax.optimization_barrier(
        (mine, near, straight, relayed, to_relay, others, acc, hold)
    )
    others = [to_relay, *others]
    back = [onward(hold[m], lambda p, c: p - (2 * m + 1 + c)) for m in range(hops // 2)]
    keep_low, give_low = carries(0, mine, near, straight, others)
    keep, give = carries(1, mine, near, relayed, others)
    given_low, given = swap(give_low), swap(give)
    acc = across_sums(0, core, *pinned[:2], decays, keep_low, acc)
    acc = across_sums(1, core, *pinned[:2], decays, keep, acc)

    def outputs(half, after, keep, given, done=()):
        _, core_then = lax.optimization_barrier((after, core))
        return across_outputs(
            half, "yx", core_then, state_write, state_read, decays, keep, given, y, dx, done
        )

    position = lax.axis_index("head").astype(jnp.int32)
    ranks = lax.axis_size("head")

    def side_at(step):
        return lax.rem(position // step, 2).reshape(1)

    step = ranks // 2
    kept, away = given_sums(
        other, side_at(step), *pinned[:2], decays, given_low, given, acc
    )
    done = ()
    for half in range(ranks.bit_length() - 1):
        moved = lax.ppermute(away, "head", [(i, i ^ step) for i in range(ranks)])
        if half < 2:
            states_of = ((keep_low, given_low), (keep, given))[half]
            done = outputs(half, kept, *states_of, done)
            moved, done, back = lax.optimization_barrier((moved, done, back))
            if half == 0:
                swapped = swap(partner_part(other, upper, back))
            else:
                moved, done, swapped = lax.optimization_barrier((moved, done, swapped))
        step //= 2
        if step:
            kept, away = fold(side_at(step), kept, moved)

    grads = finish(core, own, swapped, kept, moved, back)
    return (attn_out, done[0], grad_q, grads[0], grads[1], done[1], grads[2], grads[3])


def solution(mesh):
    tokens = P("ctx", "head")
    shared = P("ctx", None)
    in_specs = (
        tokens,
        tokens,
        tokens,
        tokens,
        P("ctx"),
        tokens,
        shared,
        shared,
        tokens,
        tokens,
    )
    out_specs = (tokens,) * 6 + (P(("ctx", "head"), None),) * 2
    return jax.shard_map(body, mesh=mesh, in_specs=in_specs, out_specs=out_specs, check_vma=False)
```

```python
import jax
import jax.numpy as jnp
from jax import lax
from jax.experimental import pallas as pl
from jax.experimental.pallas import tpu as pltpu
from jax.sharding import PartitionSpec as P

HD = 128
P_SIZE = 64
N = 256
AUX = 16
GROUP = 8
WIDTH = GROUP * P_SIZE
FLOOR = -1e30
F32 = jnp.float32
BF16 = jnp.bfloat16
highest = lax.Precision.HIGHEST
BRIEF = pl.CostEstimate(flops=1, bytes_accessed=1, transcendentals=0)


SCALAR = pl.BlockSpec(memory_space=pltpu.SMEM)
WHOLE = pl.BlockSpec(memory_space=pltpu.VMEM)
ANYWHERE = pl.BlockSpec(memory_space=pl.ANY)


def dot(a, b):
    return jnp.dot(a, b, preferred_element_type=F32)


def dot_nt(a, b):
    return lax.dot_general(a, b, (((1,), (1,)), ((), ())), preferred_element_type=F32)


def flip(a):
    return a.astype(F32).T.astype(BF16)


def running_decay(ld):
    rows = ld.shape[1]
    upper = lax.broadcasted_iota(jnp.int32, (rows, rows), 0) <= lax.broadcasted_iota(
        jnp.int32, (rows, rows), 1
    )
    return jnp.dot(ld, upper.astype(F32), preferred_element_type=F32, precision=highest)


def doc_row_col(doc_ref):
    row = doc_ref[...].astype(F32) + 1.0
    rows = row.shape[1]
    grid = jnp.broadcast_to(row, (rows, rows))
    return row, grid.T


def split(value):
    high = value.astype(BF16)
    return high, (value - high.astype(F32)).astype(BF16)


def spread(heads, first_head):
    row = lax.broadcasted_iota(jnp.int32, (heads, WIDTH), 0)
    col = lax.broadcasted_iota(jnp.int32, (heads, WIDTH), 1)
    return (lax.shift_right_logical(col, 6) + first_head == row).astype(F32).astype(BF16)


def params(mib):
    return pltpu.CompilerParams(vmem_limit_bytes=mib * 1024 * 1024)


def aux_block(decay, leaving, far):
    high, low = split(decay)
    place = lax.broadcasted_iota(jnp.int32, (AUX, decay.shape[1]), 0)
    wide = jnp.where(place == 0, high.astype(F32), low.astype(F32))
    return jnp.where(
        place < 2, wide, jnp.where(place == 2, leaving, jnp.where(place == 3, far, 0.0))
    ).astype(BF16)


def aux_rows(part):
    part = part.astype(F32)
    return part[0:1] + part[1:2], part[2:3], part[3:4]


def states_kernel(kind, x, dy, b, c, ld, doc, *refs):
    keys, values, out, packet = refs[:4] if len(refs) > 6 else (None, None, refs[0], None)
    z_in, side, ld_in, doc_in, sems = refs[-5:]
    heads = ld.shape[0]
    cols = out.shape[1]
    forward = kind[0] == 0
    part = min(cols, 2 * WIDTH)

    def copies(z, matrix):
        yield pltpu.make_async_copy(matrix, side, sems.at[2])
        for k in range(cols // part):
            to = pl.ds(k * part, part)
            source = z.at[:, pl.ds(k * part, part)]
            yield pltpu.make_async_copy(source, z_in.at[:, to], sems.at[3 + k])

    small = [
        pltpu.make_async_copy(ld, ld_in, sems.at[0]),
        pltpu.make_async_copy(doc, doc_in, sems.at[1]),
    ]
    for copy in small:
        copy.start()
    if packet is not None:
        rows, width = keys.shape
        moves = [
            pltpu.make_async_copy(part, packet.at[pl.ds(0, rows), pl.ds(k * width, width)], sem)
            for k, (part, sem) in enumerate(((keys, sems.at[sems.shape[0] - 2]), (values, sems.at[sems.shape[0] - 1])))
        ]
        for copy in moves:
            copy.start()

    @pl.when(forward)
    def _():
        for copy in copies(x, b):
            copy.start()

    @pl.when(jnp.logical_not(forward))
    def _():
        for copy in copies(dy, c):
            copy.start()

    large = list(copies(x, b))
    for copy in small:
        copy.wait()
    row, col = doc_row_col(doc_in)
    first = jnp.min(row, axis=1, keepdims=True)
    last = jnp.max(row, axis=1, keepdims=True)
    leaving, far = jnp.where(forward, last, first), jnp.where(forward, first, last)
    cum = running_decay(ld_in[...]).T
    end = cum[-1:, :]
    gap = jnp.where(forward, end - cum, cum)
    weight = jnp.where(col[:, :heads] == leaving, jnp.exp(gap), 0.0).astype(BF16)
    high, low = split(jnp.exp(jnp.broadcast_to(end, (8, heads))))
    large[0].wait()
    turned = flip(side[...])
    for t in range(cols // WIDTH):
        if t * WIDTH % part == 0:
            large[1 + t * WIDTH // part].wait()
        at = slice(t * WIDTH, (t + 1) * WIDTH)
        e = spread(heads, t * GROUP)
        z = (z_in[:, at].astype(F32) * dot(weight, e)).astype(BF16)
        out[:N, at] = dot(turned, z).astype(BF16)
        decay = dot(high, e) + dot(low, e)
        out[N:, at] = aux_block(decay[0:1], leaving, far)
    if packet is not None:
        for copy in moves:
            copy.wait()
        docs = jnp.concatenate([row] * (2 * width // rows), axis=1)
        packet[rows:, :] = jnp.broadcast_to(docs, (AUX, 2 * width)).astype(BF16)


def states(kind, x, dy, b, c, ld, doc, kv=()):
    rows, cols = x.shape
    heads = ld.shape[0]
    hbm = pl.BlockSpec(memory_space=pltpu.HBM)
    whole = lambda a: pl.BlockSpec(a.shape, lambda j, s: (0,) * a.ndim)
    shapes = [jax.ShapeDtypeStruct((N + AUX, cols), BF16)]
    if kv:
        shapes.append(jax.ShapeDtypeStruct((rows + AUX, 2 * kv[0].shape[1]), BF16))

    return pl.pallas_call(
        states_kernel,
        grid_spec=pltpu.PrefetchScalarGridSpec(
            num_scalar_prefetch=1,
            grid=(1,),
            in_specs=[hbm] * (6 + len(kv)),
            out_specs=[whole(a) for a in shapes],
            scratch_shapes=[
                pltpu.VMEM((rows, cols), BF16),
                pltpu.VMEM((rows, N), BF16),
                pltpu.VMEM((heads, rows), F32),
                pltpu.VMEM((1, rows), jnp.int32),
                pltpu.SemaphoreType.DMA((5 + max(1, cols // (2 * WIDTH)),)),
            ],
        ),
        out_shape=shapes,
        compiler_params=params(10),
        cost_estimate=BRIEF,
        name="chunk_states",
    )(kind, x, dy, b, c, ld, doc, *kv)


def merge_kernel(mine, got, out, low):
    cols = out.shape[2]
    for t in range(2 * cols // WIDTH):
        at = slice(t * WIDTH, (t + 1) * WIDTH)
        half, first = t * WIDTH // cols, t * WIDTH // cols * cols
        to = slice(t * WIDTH - first, (t + 1) * WIDTH - first)
        decay, leaving, far = aux_rows(mine[N:, at])
        decay_got, leaving_got, far_got = aux_rows(got[N:, at])
        linked = (leaving_got == far_got) & (leaving == far_got)
        total = jnp.where(linked, decay_got, 0.0) * mine[:N, at].astype(F32)
        total = (got[:N, at].astype(F32) + total).astype(BF16)
        aux = aux_block(decay * decay_got, leaving_got, far)
        out[half, :N, to] = total
        out[half, N:, to] = aux
        if half == 0:
            low[:N, to] = total
            low[N:, to] = aux


def merge(mine, got):
    rows, cols = mine.shape
    return pl.pallas_call(
        merge_kernel,
        out_shape=[
            jax.ShapeDtypeStruct((2, rows, cols // 2), BF16),
            jax.ShapeDtypeStruct((rows, cols // 2), BF16),
        ],
        compiler_params=params(4),
        cost_estimate=BRIEF,
        name="pair_merge",
    )(mine, got)


def carry_kernel(half, mine, near, extra, *refs):
    (relay, *others), (keep, out, send, sems) = refs[:-4], refs[-4:]
    cols = keep.shape[1]
    span, copies = min(cols, 2 * WIDTH), []
    for t in range(cols // WIDTH):
        at = slice(t * WIDTH, (t + 1) * WIDTH)
        own = slice(half * cols + t * WIDTH, half * cols + (t + 1) * WIDTH)
        here = near[half, :, at].astype(F32) + extra[:, at].astype(F32)
        total, coefficient, now = here[:N], None, aux_rows(here[N:])
        entering = now[1]
        for k, part in enumerate(others):
            there = part[half, :, at].astype(F32)
            if k == 0:
                there = there + relay[half, :, at].astype(F32)
            after = aux_rows(there[N:])
            step = jnp.where((now[1] == now[2]) & (after[1] == now[2]), now[0], 0.0)
            coefficient = step if coefficient is None else coefficient * step
            total = total + coefficient * there[:N]
            now = after
        decay, leaving, far = aux_rows(mine[N:, own])
        linked = (leaving == far) & (entering == far)
        passed = mine[:N, own].astype(F32) + jnp.where(linked, decay, 0.0) * total
        keep[:N, at] = total.astype(BF16)
        keep[N:, at] = aux_block(jnp.zeros_like(decay), entering, entering)
        send[:N, at] = passed.astype(BF16)
        send[N:, at] = aux_block(jnp.zeros_like(decay), leaving, leaving)
        if (t + 1) * WIDTH % span == 0:
            n = (t + 1) * WIDTH // span - 1
            piece = (slice(None), pl.ds(n * span, span))
            copies.append(pltpu.make_async_copy(send.at[piece], out.at[piece], sems.at[n]))
            copies[-1].start()
    for copy in copies:
        copy.wait()


def carries(half, mine, near, extra, others):
    out = pltpu.VMEM(extra.shape, BF16)

    def kernel(*refs):
        carry_kernel(half, *refs)

    return pl.pallas_call(
        kernel,
        in_specs=[WHOLE] * (3 + len(others)),
        out_specs=[WHOLE, ANYWHERE],
        out_shape=[out, jax.ShapeDtypeStruct(extra.shape, BF16)],
        scratch_shapes=[pltpu.VMEM(extra.shape, BF16), pltpu.SemaphoreType.DMA((4,))],
        compiler_params=params(6),
        cost_estimate=BRIEF,
        name="carry_states",
    )(mine, near, extra, *others)


def inside_kernel(
    x, dy, b, c, ld, doc, y, dx, acc, decays, cum_col, cum_row, gram, gram_t, veil, veil_t, total
):
    j = pl.program_id(0)
    heads, rows = ld.shape
    here = x.shape[1] // P_SIZE

    @pl.when(j == 0)
    def _():
        across_tokens = running_decay(ld[...])
        cum_row[...] = across_tokens
        cum = across_tokens.T
        for k in range(heads // here):
            cum_col[k] = cum[:, k * here : (k + 1) * here]
        row, col = doc_row_col(doc)
        decays[0] = jnp.exp(cum)
        decays[1] = jnp.exp(cum[-1:, :] - cum)
        decays[2] = col[:, :heads]
        places = [lax.broadcasted_iota(jnp.int32, (rows, rows), k) for k in range(2)]
        same = col == row
        veil[...] = jnp.where(same & (places[0] >= places[1]), 0.0, FLOOR)
        veil_t[...] = jnp.where(same & (places[0] <= places[1]), 0.0, FLOOR)
        gram[...] = dot_nt(c[...], b[...])
        gram_t[...] = dot_nt(b[...], c[...])
        total[...] = jnp.zeros_like(total)

    lane = lax.broadcasted_iota(jnp.int32, (1, 2 * P_SIZE), 1)
    left = (lane < P_SIZE).astype(F32).astype(BF16)
    right = (lane >= P_SIZE).astype(F32).astype(BF16)
    col_block = cum_col[j]
    row_block = cum_row[pl.ds(pl.multiple_of(j * here, here), here), :]
    for pair in range(here // 2):
        at = slice(pair * 2 * P_SIZE, (pair + 1) * 2 * P_SIZE)
        x_pair, y_pair = x[:, at], dy[:, at]
        x_both = jnp.concatenate([x_pair * left, x_pair * right], axis=0)
        y_both = jnp.concatenate([y_pair * left, y_pair * right], axis=0)
        inner = dot_nt(y_both, x_pair)
        mixed, turned, sums = [], [], 0.0
        for k in range(2):
            head = 2 * pair + k
            gap = col_block[:, head : head + 1] - row_block[head : head + 1, :]
            decay = jnp.exp(gap + veil[...])
            sums = sums + decay * inner[k * rows : (k + 1) * rows]
            mixed.append((decay * gram[...]).astype(BF16))
            turned.append((jnp.exp(veil_t[...] - gap) * gram_t[...]).astype(BF16))
        total[...] += sums
        y[:, at] = dot(jnp.concatenate(mixed, axis=1), x_both).astype(BF16)
        dx[:, at] = dot(jnp.concatenate(turned, axis=1), y_both).astype(BF16)

    @pl.when(j == pl.num_programs(0) - 1)
    def _():
        weighted = total[...]
        acc[0] = dot(weighted.T.astype(BF16), c[...])
        acc[1] = dot(weighted.astype(BF16), b[...])


def inside(x, dy, b, c, ld, doc):
    rows, cols = x.shape
    heads = ld.shape[0]
    span = min(cols, 4 * WIDTH)
    here = span // P_SIZE
    whole = lambda a: pl.BlockSpec(a.shape, lambda j: (0,) * a.ndim)
    block = pl.BlockSpec((rows, span), lambda j: (0, j))
    shapes = [
        jax.ShapeDtypeStruct((rows, cols), BF16),
        jax.ShapeDtypeStruct((rows, cols), BF16),
        jax.ShapeDtypeStruct((2, rows, N), F32),
        jax.ShapeDtypeStruct((3, rows, heads), F32),
    ]
    square = pltpu.VMEM((rows, rows), F32)
    return pl.pallas_call(
        inside_kernel,
        grid=(cols // span,),
        in_specs=[block, block, whole(b), whole(c), whole(ld), whole(doc)],
        out_specs=[block, block, whole(shapes[2]), whole(shapes[3])],
        out_shape=shapes,
        scratch_shapes=[
            pltpu.VMEM((heads // here, rows, here), F32),
            pltpu.VMEM((heads, rows), F32),
            *[square] * 5,
        ],
        compiler_params=params(10),
        cost_estimate=BRIEF,
        name="inside_chunk",
    )(x, dy, b, c, ld, doc)


def carried_weight(forward, carried, decays):
    doc = carried[N:, :HD].astype(F32)[2:3, 0:1]
    decay = jnp.where(forward, decays[0], decays[1])
    return jnp.where(decays[2] == doc, decay, 0.0).astype(BF16)


def begin(picked, one, two, target, sem):
    copies = [pltpu.make_async_copy(source, target, sem) for source in (one, two)]

    @pl.when(picked)
    def _():
        copies[1].start()

    @pl.when(jnp.logical_not(picked))
    def _():
        copies[0].start()

    return copies[0]


def sums_kernel(kind, x, dy, decays, low, high, acc_in, acc, z_in, sems):
    heads = decays.shape[2]
    cols = x.shape[1]
    part = min(cols // 2, 2 * WIDTH)
    forward = kind[0] == 0
    waits = []
    for n in range(cols // part):
        piece = (slice(None), pl.ds(n * part, part))
        waits.append(begin(forward, x.at[piece], dy.at[piece], z_in.at[piece], sems.at[n]))
    weight = carried_weight(forward, low, decays)
    total = 0.0
    for t in range(cols // WIDTH):
        if t * WIDTH % part == 0:
            waits[t * WIDTH // part].wait()
        half, first = t * WIDTH // (cols // 2), t * WIDTH % (cols // 2)
        z = z_in[:, t * WIDTH : (t + 1) * WIDTH].astype(F32)
        z = (z * dot(weight, spread(heads, t * GROUP))).astype(BF16)
        total = total + dot_nt(z, (low, high)[half][:N, first : first + WIDTH])
    acc[0] = acc_in[0] + jnp.where(forward, 0.0, total)
    acc[1] = acc_in[1] + jnp.where(forward, total, 0.0)


def divide(side, acc, kept, away):
    rows = kept.shape[1]
    kept[...] = acc[:, pl.ds(pl.multiple_of(side[0] * rows, rows), rows), :]
    away[...] = acc[:, pl.ds(pl.multiple_of((1 - side[0]) * rows, rows), rows), :].astype(BF16)


def halves(acc):
    shape = (acc.shape[0], acc.shape[1] // 2, acc.shape[2])
    return [jax.ShapeDtypeStruct(shape, F32), jax.ShapeDtypeStruct(shape, BF16)]


def across_sums(kind, x, dy, decays, low, high, acc):
    return pl.pallas_call(
        sums_kernel,
        in_specs=[SCALAR, ANYWHERE, ANYWHERE] + [WHOLE] * 4,
        out_specs=WHOLE,
        out_shape=jax.ShapeDtypeStruct(acc.shape, F32),
        scratch_shapes=[pltpu.VMEM(x.shape, BF16), pltpu.SemaphoreType.DMA((8,))],
        compiler_params=params(7),
        cost_estimate=BRIEF,
        name="across_sums",
    )(kind, x, dy, decays, low, high, acc)


def fetch_given(sources, buffer, sems):
    part = min(sources[0].shape[1], 2 * WIDTH)
    waits, place = [], 0
    for source in sources:
        for first in range(0, source.shape[1], part):
            piece = source.at[:, pl.ds(first, part)]
            target = buffer.at[:, pl.ds(place, part)]
            waits.append(pltpu.make_async_copy(piece, target, sems.at[place // part]))
            waits[-1].start()
            place += part
    return waits, part


def given_kernel(
    kind, side, x, dy, decays, acc_in, low, high, kept, away, acc, carried, sems, z_in, z_sems
):
    heads = decays.shape[2]
    forward = kind[0] == 0
    waits, part = fetch_given((low, high), carried, sems)
    z_waits = []
    for n in range(len(waits)):
        piece = (slice(None), pl.ds(n * part, part))
        z_waits.append(begin(forward, x.at[piece], dy.at[piece], z_in.at[piece], z_sems.at[n]))
    total = 0.0
    for t in range(carried.shape[1] // WIDTH):
        if t * WIDTH % part == 0:
            waits[t * WIDTH // part].wait()
            z_waits[t * WIDTH // part].wait()
        if t == 0:
            weight = carried_weight(forward, carried, decays)
        at = slice(t * WIDTH, (t + 1) * WIDTH)
        z = z_in[:, at].astype(F32)
        z = (z * dot(weight, spread(heads, t * GROUP))).astype(BF16)
        total = total + dot_nt(z, carried[:N, at])
    acc[0] = acc_in[0] + jnp.where(forward, 0.0, total)
    acc[1] = acc_in[1] + jnp.where(forward, total, 0.0)
    divide(side, acc, kept, away)


def given_sums(kind, side, x, dy, decays, low, high, acc):
    return pl.pallas_call(
        given_kernel,
        in_specs=[SCALAR, SCALAR, ANYWHERE, ANYWHERE, WHOLE, WHOLE, ANYWHERE, ANYWHERE],
        out_specs=[WHOLE, WHOLE],
        out_shape=halves(acc),
        scratch_shapes=[
            pltpu.VMEM(acc.shape, F32),
            pltpu.VMEM((low.shape[0], 2 * low.shape[1]), BF16),
            pltpu.SemaphoreType.DMA((8,)),
            pltpu.VMEM(x.shape, BF16),
            pltpu.SemaphoreType.DMA((8,)),
        ],
        compiler_params=params(8),
        cost_estimate=BRIEF,
        name="given_sums",
    )(kind, side, x, dy, decays, acc, low, high)


def fold_kernel(side, kept_in, moved, kept, away, acc):
    acc[...] = kept_in[...] + moved[...].astype(F32)
    divide(side, acc, kept, away)


def fold(side, kept, moved):
    return pl.pallas_call(
        fold_kernel,
        in_specs=[SCALAR, WHOLE, WHOLE],
        out_specs=[WHOLE, WHOLE],
        out_shape=halves(kept),
        scratch_shapes=[pltpu.VMEM(kept.shape, F32)],
        compiler_params=params(2),
        cost_estimate=BRIEF,
        name="sums_fold",
    )(side, kept, moved)


def outputs_kernel(half, wanted, core, b, c, decays, keep, source, y_in, dx_in, *refs):
    outs, (buffer, sems, given, arrivals) = refs[-4 - len(wanted) : -4], refs[-4:]
    waits, piece = fetch_given((source,), given, arrivals)
    heads = decays.shape[2]
    cols = keep.shape[1]
    lower = core[0] == 0
    part = min(cols, 2 * WIDTH)
    copies, weights = [], {}
    for t in range(cols // WIDTH):
        if t * WIDTH % piece == 0:
            waits[t * WIDTH // piece].wait()
        at = slice(t * WIDTH, (t + 1) * WIDTH)
        to = slice(half * cols + t * WIDTH, half * cols + (t + 1) * WIDTH)
        e = spread(heads, half * (heads // 2) + t * GROUP)
        for out, name in zip(outs, wanted):
            k = "yx".index(name)
            carried = (keep, given) if k == 0 else (given, keep)
            side, old, decay = ((c, y_in, decays[0]), (b, dx_in, decays[1]))[k]
            if t == 0:
                docs = [part_of[N:, :HD].astype(F32)[2:3, 0:1] for part_of in carried]
                doc = jnp.where(lower, docs[0], docs[1])
                weights[k] = jnp.where(decays[2] == doc, decay, 0.0).astype(BF16)
            state = jnp.where(lower, carried[0][:N, at], carried[1][:N, at])
            term = dot(weights[k], e) * dot(side[...], state)
            buffer[k, :, at] = (old[:, to].astype(F32) + term).astype(BF16)
            if (t + 1) * WIDTH % part == 0:
                n = (t + 1) * WIDTH // part - 1
                source_part = buffer.at[k, :, pl.ds(n * part, part)]
                target = out.at[:, pl.ds(half * cols + n * part, part)]
                copies.append(pltpu.make_async_copy(source_part, target, sems.at[k, n]))
                copies[-1].start()
    for copy in copies:
        copy.wait()


def across_outputs(half, wanted, core, b, c, decays, keep, given, y, dx, done=()):
    rows, cols = y.shape
    parts = max(1, cols // 2 // (2 * WIDTH))
    anywhere = pl.BlockSpec(memory_space=pl.ANY)

    def kernel(*refs):
        outputs_kernel(half, wanted, *refs)

    return pl.pallas_call(
        kernel,
        in_specs=[SCALAR] + [WHOLE] * 4 + [ANYWHERE] + [WHOLE] * 2 + [anywhere for _ in done],
        out_specs=[anywhere for _ in wanted],
        out_shape=[jax.ShapeDtypeStruct(y.shape, BF16) for _ in wanted],
        scratch_shapes=[
            pltpu.VMEM((2, rows, cols // 2), BF16),
            pltpu.SemaphoreType.DMA((2, parts)),
            pltpu.VMEM(given.shape, BF16),
            pltpu.SemaphoreType.DMA((4,)),
        ],
        input_output_aliases={8 + k: k for k in range(len(done))},
        compiler_params=params(8),
        cost_estimate=BRIEF,
        name="across_outputs",
    )(core, b, c, decays, keep, given, y, dx, *done)


def partner_kernel(other, upper, *refs):
    parts, out = refs[:-1], refs[-1]
    out[...] = (
        sum(part[pl.ds(other[0], 1)][0].astype(F32) for part in parts) + upper[...].astype(F32)
    ).astype(BF16)


def partner_part(other, upper, parts):
    return pl.pallas_call(
        partner_kernel,
        in_specs=[SCALAR] + [WHOLE] * (1 + len(parts)),
        out_specs=WHOLE,
        out_shape=jax.ShapeDtypeStruct(upper.shape, BF16),
        compiler_params=params(2),
        cost_estimate=BRIEF,
        name="partner_part",
    )(other, upper, *parts)


def finish_kernel(core, own, swapped, kept, moved, *refs):
    parts, (grad_k, grad_v, grad_b, grad_c) = refs[:-4], refs[-4:]
    cols = grad_k.shape[1]
    total = own[...] + swapped[...].astype(F32)
    total = total + sum(part[pl.ds(core[0], 1)][0].astype(F32) for part in parts)
    grad_k[...] = total[:, :cols].astype(BF16)
    grad_v[...] = total[:, cols:].astype(BF16)
    grad_b[...] = (kept[0] + moved[0].astype(F32)).astype(BF16)
    grad_c[...] = (kept[1] + moved[1].astype(F32)).astype(BF16)


def finish(core, own, swapped, kept, moved, parts):
    rows, cols = own.shape
    key = jax.ShapeDtypeStruct((rows, cols // 2), BF16)
    shared = jax.ShapeDtypeStruct(kept.shape[1:], BF16)
    return pl.pallas_call(
        finish_kernel,
        in_specs=[SCALAR] + [WHOLE] * (4 + len(parts)),
        out_shape=[key, key, shared, shared],
        compiler_params=params(2),
        cost_estimate=BRIEF,
        name="last_sums",
    )(core, own, swapped, kept, moved, *parts)


def key_blocks(lower, packet, partner, far, other, reach):
    blocks = [packet[...]]
    for k in range(1, reach + 1):
        if k % 2 == 0:
            blocks.append(far[k // 2 - 1][...])
        else:
            up = partner if k == 1 else other[k // 2 - 1]
            blocks.append(jnp.where(lower, other[k // 2][...], up[...]))
    return blocks


def attention_kernel(reach, group, kv_local, core, q, do, doc, packet, partner, *refs):
    count = len(refs) - 6 - 5
    far, other = refs[: count // 2], refs[count // 2 : count]
    o, dq, own, hold, send, upper = refs[count : count + 6]
    keys, values, veil, probs, grads = refs[count + 6 :]
    lower = core[0] == 0
    rows = q.shape[0]
    scale = HD ** (-0.5)
    row, _ = doc_row_col(doc)
    packets = key_blocks(lower, packet, partner, far, other, reach)
    for k, block in enumerate(packets):
        at = slice(k * rows, (k + 1) * rows)
        key_row = block[rows:, :HD].astype(F32)[0:1, :]
        seen = jnp.broadcast_to(key_row, (rows, rows)).T == row
        if k == 0:
            seen = seen & (
                lax.broadcasted_iota(jnp.int32, (rows, rows), 0)
                <= lax.broadcasted_iota(jnp.int32, (rows, rows), 1)
            )
        veil[at, :] = jnp.where(seen, 0.0, FLOOR)
        for g in range(kv_local):
            keys[g, at, :] = block[:rows, g * HD : (g + 1) * HD]
            values[g, at, :] = block[:rows, (kv_local + g) * HD : (kv_local + g + 1) * HD]
    for g in range(kv_local):
        k_all, v_all = keys[g], values[g]
        k_turned, v_turned = flip(k_all), flip(v_all)
        dk = dv = 0.0
        for h in range(0, group, 2):
            ats = [slice((g * group + h + i) * HD, (g * group + h + i + 1) * HD) for i in range(2)]
            q_two = jnp.concatenate([q[:, at] for at in ats], axis=0)
            do_two = jnp.concatenate([do[:, at] for at in ats], axis=0)
            do_turned = do_two.astype(F32).T
            mask = jnp.concatenate([veil[...]] * 2, axis=1)
            scores = dot(k_all, flip(q_two)) * scale + mask
            top = jnp.max(scores, axis=0, keepdims=True)
            weights = jnp.exp(scores - top)
            over = 1.0 / jnp.sum(weights, axis=0, keepdims=True)
            out = (dot(v_turned, weights.astype(BF16)) * over).astype(BF16).astype(F32)
            inner = jnp.sum(do_turned * out, axis=0, keepdims=True)
            prob = weights * over
            prob_grad = dot(v_all, do_turned.astype(BF16))
            dscore = (prob * (prob_grad - inner)).astype(BF16)
            probs[...] = prob.astype(BF16)
            grads[...] = dscore
            dq_turned = dot(k_turned, dscore) * scale
            for i, at in enumerate(ats):
                o[:, at] = out[:, i * rows : (i + 1) * rows].T.astype(BF16)
                dq[:, at] = dq_turned[:, i * rows : (i + 1) * rows].T.astype(BF16)
            dk = dk + dot(grads[...], q_two)
            dv = dv + dot(probs[...], do_two)
        for part, col in ((dk * scale, g), (dv, kv_local + g)):
            cols = slice(col * HD, (col + 1) * HD)
            own[:, cols] = part[:rows]

            def of(k):
                return part[k * rows : (k + 1) * rows] if k <= reach else jnp.zeros((rows, HD), F32)

            upper[:, cols] = jnp.where(lower, 0.0, of(1)).astype(BF16)
            for m in range(reach // 4):
                odd, even = 2 * m + 1, 2 * m + 2
                for place in range(2):
                    low_odd, up_odd = of(2 * odd - place), of(2 * odd + 1 - place)
                    low_even, up_even = of(2 * even - place), of(2 * even + 1 - place)
                    hold[m, place, :, cols] = jnp.where(lower, low_odd, up_even).astype(BF16)
                    send[m, place, :, cols] = jnp.where(lower, low_even, up_odd).astype(BF16)


def attention(core, q, do, doc, packet, partner, far, other, reach):
    rows, cols = q.shape
    kv_cols = packet.shape[1]
    kv_local = kv_cols // (2 * HD)
    group = cols // (kv_local * HD)
    blocks = reach + 1
    args = (q, do, doc, packet, partner, *far, *other)

    def kernel(*refs):
        attention_kernel(reach, group, kv_local, *refs)

    whole = lambda a: pl.BlockSpec(a.shape, lambda j, s: (0,) * a.ndim)
    shapes = [
        jax.ShapeDtypeStruct((rows, cols), BF16),
        jax.ShapeDtypeStruct((rows, cols), BF16),
        jax.ShapeDtypeStruct((rows, kv_cols), F32),
        jax.ShapeDtypeStruct((reach // 4, 2, rows, kv_cols), BF16),
        jax.ShapeDtypeStruct((reach // 4, 2, rows, kv_cols), BF16),
        jax.ShapeDtypeStruct((rows, kv_cols), BF16),
    ]
    return pl.pallas_call(
        kernel,
        grid_spec=pltpu.PrefetchScalarGridSpec(
            num_scalar_prefetch=1,
            grid=(1,),
            in_specs=[whole(a) for a in args],
            out_specs=[whole(a) for a in shapes],
            scratch_shapes=[
                pltpu.VMEM((kv_local, blocks * rows, HD), BF16),
                pltpu.VMEM((kv_local, blocks * rows, HD), BF16),
                pltpu.VMEM((blocks * rows, rows), F32),
                pltpu.VMEM((blocks * rows, 2 * rows), BF16),
                pltpu.VMEM((blocks * rows, 2 * rows), BF16),
            ],
        ),
        out_shape=shapes,
        compiler_params=params(14),
        cost_estimate=BRIEF,
        name="packed_attention",
    )(core, *args)


def shift(x, axis, by):
    count = lax.axis_size(axis)
    hops = [(i, i + by) for i in range(count) if 0 <= i + by < count]
    return lax.ppermute(x, axis, hops)


def swap(x):
    count = lax.axis_size("ctx")
    return lax.ppermute(x, "ctx", [(i, i ^ 1) for i in range(count)])


def onward(x, route):
    pairs = lax.axis_size("ctx") // 2
    hops = [(2 * p + c, 2 * route(p, c) + c) for p in range(pairs) for c in range(2)]
    return lax.ppermute(x, "ctx", [(i, k) for i, k in hops if 0 <= k < 2 * pairs])


NOWHERE = -1


def ahead(by):
    return lambda p, c: p + by * (1 - 2 * c)


def ahead_in_row(p, c):
    return ahead(1)(p, c) if p % 2 == c else NOWHERE


def ahead_to_relay(p, c):
    return ahead(2)(p, c) if p % 2 != c else NOWHERE


def ahead_direct(p, c):
    return ahead(2)(p, c) if p % 2 == c else NOWHERE


def ahead_across(p, c):
    return ahead(1)(p, c) if p % 2 != c else NOWHERE


def ahead_by_relay(pairs):
    def route(p, c):
        source = p - 2 * (1 - 2 * c)
        relayed = p % 2 != c and 0 <= source < pairs
        return p - (1 - 2 * c) if relayed else NOWHERE

    return route


def body(
    queries,
    keys_in,
    values_in,
    attn_cotan,
    doc_ids,
    ssd_input,
    state_write,
    state_read,
    log_decay,
    ssd_cotan,
):
    rows = doc_ids.shape[0]
    kv_cols = keys_in.shape[1]
    devices = lax.axis_size("ctx")
    pairs = devices // 2
    hops = pairs // 2
    reach = 2 * hops
    doc = doc_ids.reshape(1, rows)
    core = lax.rem(lax.axis_index("ctx"), 2).astype(jnp.int32).reshape(1)
    other = 1 - core

    args = (ssd_input, ssd_cotan, state_write, state_read, log_decay.T, doc)
    pinned = [pltpu.with_memory_space_constraint(a, pltpu.HBM) for a in args]
    kv = [pltpu.with_memory_space_constraint(a, pltpu.HBM) for a in (keys_in, values_in)]
    sent, packet = states(other, *pinned, kv=kv)
    got = swap(sent)
    (mine,) = states(core, *pinned)
    far = [shift(packet, "ctx", 2 * k) for k in range(1, hops + 1)]
    far, mine = lax.optimization_barrier((far, mine))
    pair, low = merge(mine, got)
    near = onward(pair, ahead_in_row)
    to_relay = onward(pair, ahead_to_relay)
    others = [onward(pair, ahead_direct)]
    others += [onward(pair, ahead(k)) for k in range(3, hops + 1)]
    partner = swap(packet)
    far_other = [swap(part) for part in far]

    _, doc_then = lax.optimization_barrier((pair, doc))
    y, dx, acc, decays = inside(*args[:5], doc_then)
    _, core_then = lax.optimization_barrier((acc, core))
    attn_out, grad_q, own, hold, send, upper = attention(
        core_then, queries, attn_cotan, doc, packet, partner, far, far_other, reach
    )
    low, own = lax.optimization_barrier((low, own))
    straight = onward(low, ahead_across)
    relayed = onward(to_relay[1], ahead_by_relay(pairs))
    near, send = lax.optimization_barrier((near, send))
    hold = (hold.astype(F32) + swap(send).astype(F32)).astype(BF16)

    mine, near, straight, relayed, to_relay, others, acc, hold = lax.optimization_barrier(
        (mine, near, straight, relayed, to_relay, others, acc, hold)
    )
    others = [to_relay, *others]
    back = [onward(hold[m], lambda p, c: p - (2 * m + 1 + c)) for m in range(hops // 2)]
    keep_low, give_low = carries(0, mine, near, straight, others)
    keep, give = carries(1, mine, near, relayed, others)
    given_low, given = swap(give_low), swap(give)
    acc = across_sums(core, *pinned[:2], decays, keep_low, keep, acc)

    def outputs(half, after, keep, given, done=()):
        _, core_then = lax.optimization_barrier((after, core))
        return across_outputs(
            half, "yx", core_then, state_write, state_read, decays, keep, given, y, dx, done
        )

    position = lax.axis_index("head").astype(jnp.int32)
    ranks = lax.axis_size("head")

    def side_at(step):
        return lax.rem(position // step, 2).reshape(1)

    step = ranks // 2
    kept, away = given_sums(
        other, side_at(step), *pinned[:2], decays, given_low, given, acc
    )
    done = ()
    for half in range(ranks.bit_length() - 1):
        moved = lax.ppermute(away, "head", [(i, i ^ step) for i in range(ranks)])
        if half < 2:
            states_of = ((keep_low, given_low), (keep, given))[half]
            done = outputs(half, kept, *states_of, done)
            moved, done, back = lax.optimization_barrier((moved, done, back))
            if half == 0:
                swapped = swap(partner_part(other, upper, back))
            else:
                moved, done, swapped = lax.optimization_barrier((moved, done, swapped))
        step //= 2
        if step:
            kept, away = fold(side_at(step), kept, moved)

    grads = finish(core, own, swapped, kept, moved, back)
    return (attn_out, done[0], grad_q, grads[0], grads[1], done[1], grads[2], grads[3])


def solution(mesh):
    tokens = P("ctx", "head")
    shared = P("ctx", None)
    in_specs = (
        tokens,
        tokens,
        tokens,
        tokens,
        P("ctx"),
        tokens,
        shared,
        shared,
        tokens,
        tokens,
    )
    out_specs = (tokens,) * 6 + (P(("ctx", "head"), None),) * 2
    return jax.shard_map(body, mesh=mesh, in_specs=in_specs, out_specs=out_specs, check_vma=False)
```
